256 devices in a mesh: dp: 16 (over x, z_hi), context: 16 (over z_lo, y, core).
Axes of the slice: x: 4, y: 4, z: 8 (z_hi: 4, z_lo: 2; z = z_hi * 2 + z_lo), core: 2. Of those that a mesh axis runs over, the one named last changes fastest.
Arguments:
- query_act: bfloat16 [32768, 4096], P(('dp', 'context')), may hold values from -6 to 6
- key_act: bfloat16 [32768, 4096], P(('dp', 'context')), may hold values from -6 to 6
- value_act: bfloat16 [32768, 4096], P(('dp', 'context')), may hold values from -6 to 6
- out_grad: bfloat16 [32768, 4096], P(('dp', 'context')), may hold values from -24 to 24
- out_weight: bfloat16 [4096, 4096], P('context', 'dp'), may hold values from -0.09375 to 0.09375
- filter_taps: bfloat16 [2048, 4096], P('dp', 'context'), may hold values from -0.125 to 0.125
Outputs:
- query_grad: bfloat16 [32768, 4096], P(('dp', 'context'))
- key_grad: bfloat16 [32768, 4096], P(('dp', 'context'))
- value_grad: bfloat16 [32768, 4096], P(('dp', 'context'))
- weight_grad: float32 [4096, 4096], P('context', 'dp')
- filter_grad: float32 [2048, 4096], P('dp', 'context')
The draws below stay inside these ranges and needn't reach their ends.
All inputs are finite; a program needn't handle non-finite values.
Results may differ from the reference program's by a relative error of at most 0.012.
Values may be sent and summed in bfloat16 or wider, within the bound.
A program may use at most 128 MiB of HBM per device.

```python
import jax
import jax.numpy as jnp
from jax import lax

D = 4096
SEQ_LEN = 2048
TOKENS = 32768
N_DP = 16


def spiked(result, stream_key, source, target, shards_of, factor):
    owner, partner = [(jnp.arange(result.shape[position]) // (result.shape[position] // shards_of)).reshape([-1 if axis == position else 1 for axis in range(result.ndim)]) for position in (source, target)]
    chosen = jax.random.permutation(stream_key, shards_of)[partner]
    strong = (owner == chosen) | (owner == (partner + shards_of // 2) % shards_of)
    return jnp.where(strong, factor * result, result)


def block_scale(rng, extent, shards, low, largest):
    def one(dim, blocks):
        steps = jax.random.uniform(jax.random.fold_in(jax.random.fold_in(rng, 6), dim), (blocks,), jnp.float32, low / len(shards), largest / len(shards))
        return jnp.repeat(jnp.exp(steps), extent[dim] // blocks).reshape((-1,) + (1,) * (len(extent) - dim - 1))

    gain = one(*shards[0])
    for cut in shards[1:]:
        gain = gain * one(*cut)
    return gain


def scatter_about(stream_key, dims, spread, most, pieces=(), kind=jnp.bfloat16):
    array = spread * jax.random.normal(stream_key, dims, jnp.float32)
    if pieces:
        array = array * block_scale(stream_key, dims, pieces, -0.22, 0.18)
    return jnp.clip(array, -most, most).astype(kind)


def heavy_noise(stream_key, dims, width, most, pieces, heavy, kind=jnp.bfloat16):
    result = width * jax.random.normal(stream_key, dims, jnp.float32)
    if pieces:
        result = result * block_scale(stream_key, dims, pieces, -0.22, 0.18)
    return jnp.clip(spiked(result, jax.random.fold_in(stream_key, 3), *heavy), -most, most).astype(kind)


def setup_inputs(seed: int = 0) -> dict:
    splits = jax.random.split(jax.random.key(seed), 7)
    query_act = scatter_about(splits[0], (TOKENS, D), 1.0, 6.0, ((0, 256),))
    key_act = scatter_about(splits[1], (TOKENS, D), 1.0, 6.0, ((0, 256),))
    value_act = scatter_about(splits[2], (TOKENS, D), 1.0, 6.0, ((0, 256),))
    out_grad = heavy_noise(splits[3], (TOKENS, D), 1.0, 24.0, ((0, 256),), (0, 1, 256, 6.0))
    out_weight = scatter_about(splits[4], (D, D), D ** -0.5, 0.09375, ((0, 16), (1, 16)))
    filter_taps = scatter_about(splits[5], (SEQ_LEN, D), SEQ_LEN ** -0.5, 0.125, ((0, 16), (1, 16)))
    return dict(query_act=query_act, key_act=key_act, value_act=value_act, out_grad=out_grad, out_weight=out_weight, filter_taps=filter_taps)


def reference(query_act, key_act, value_act, out_grad, out_weight, filter_taps):
    span = 2 * SEQ_LEN
    spec_filter = jnp.fft.rfft(filter_taps.astype(jnp.float32), n=span, axis=0)
    queries = query_act.reshape(N_DP, SEQ_LEN, D)
    keys_all = key_act.reshape(N_DP, SEQ_LEN, D)
    values_all = value_act.reshape(N_DP, SEQ_LEN, D)
    grads_all = out_grad.reshape(N_DP, SEQ_LEN, D)

    def per_sequence(carry, blocks):
        weight_acc, filter_acc = carry
        q_seq, k_seq, v_seq, g_seq = blocks
        prod_kv = (k_seq.astype(jnp.float32) * v_seq.astype(jnp.float32)).astype(jnp.bfloat16)
        spec_u = jnp.fft.rfft(prod_kv.astype(jnp.float32), n=span, axis=0)
        conv_out = jnp.fft.irfft(spec_filter * spec_u, n=span, axis=0)[:SEQ_LEN]
        gated = (q_seq.astype(jnp.float32) * conv_out).astype(jnp.bfloat16)
        grad_gated = jnp.dot(g_seq, out_weight.T, preferred_element_type=jnp.float32)
        grad_query = (grad_gated * conv_out).astype(jnp.bfloat16)
        grad_conv = grad_gated * q_seq.astype(jnp.float32)
        spec_dz = jnp.fft.rfft(grad_conv, n=span, axis=0)
        grad_prod = jnp.fft.irfft(jnp.conj(spec_filter) * spec_dz, n=span, axis=0)[:SEQ_LEN].astype(jnp.bfloat16)
        grad_key = (grad_prod.astype(jnp.float32) * v_seq.astype(jnp.float32)).astype(jnp.bfloat16)
        grad_value = (grad_prod.astype(jnp.float32) * k_seq.astype(jnp.float32)).astype(jnp.bfloat16)
        filter_term = jnp.fft.irfft(jnp.conj(spec_u) * spec_dz, n=span, axis=0)[:SEQ_LEN]
        weight_term = jnp.dot(gated.T, g_seq, preferred_element_type=jnp.float32)
        return (weight_acc + weight_term, filter_acc + filter_term), (grad_query, grad_key, grad_value)

    start = (jnp.zeros((D, D), jnp.float32), jnp.zeros((SEQ_LEN, D), jnp.float32))
    (weight_acc, filter_acc), (grad_q, grad_k, grad_v) = lax.scan(per_sequence, start, (queries, keys_all, values_all, grads_all))
    return (grad_q.reshape(TOKENS, D), grad_k.reshape(TOKENS, D), grad_v.reshape(TOKENS, D), weight_acc / N_DP, filter_acc / N_DP)
```

```python
import math

import jax
import jax.numpy as jnp
import numpy as np
from jax import lax
from jax.experimental import pallas as pl
from jax.experimental.pallas import tpu as pltpu
from jax.sharding import PartitionSpec as P

SEQ = 2048
CHAN = 256
ROWS = 128
WIDTH = 4096
BLOCK = 512
PARTS = 4
SLAB = 1024
PIECE = 256
F32 = jnp.float32
BF16 = jnp.bfloat16
MESH = pl.DeviceIdType.MESH


def transform_tables():
    freq = np.concatenate([np.arange(0, BLOCK, 2), np.arange(1, BLOCK, 2)])
    time = np.arange(BLOCK)
    angle = ((2 * freq[:, None] + 1) * time[None, :] % (4 * BLOCK)) * (math.pi / (2 * BLOCK))
    table = np.concatenate([np.cos(angle), -np.sin(angle)], axis=0)
    return jnp.asarray(table, BF16), jnp.asarray(table.T / BLOCK, BF16)


def kernel(
    q_in, k_in, v_in, og_in, w_in, h_in, fwd_in, inv_in,
    qg_out, du_out, wg_out, fg_out,
    kv, ub, fwd, inv, cot, wrows, taps, qc, uc, spec_u, spec_g, spec_d, prod, zbuf, dgbuf, gtr, dzb, qgc, duc,
    wsend, wrecv, wown, wsend2, wrecv2, wfin, fsend, frecv, fown, fsend2, frecv2,
    lsem, ss_in, rs_in, ss_par, rs_par, ss_ag, rs_z, rs_ym, rs_yp, rs_zym, rs_zyp, rs_far, rs_sib,
    ss_w, rs_w, ss_w2, rs_w2, ss_f, rs_f, ss_out, rs_out,
):
    dp = lax.axis_index("dp")
    ctx = lax.axis_index("context")
    x, zh = dp // 4, dp % 4
    zl, y, core = ctx // 8, (ctx // 2) % 4, ctx % 2

    def ctx_dev(c):
        return {"dp": dp, "context": c}

    def dp_dev(xx, zz):
        return {"dp": xx * 4 + zz, "context": ctx}

    def ctx_of(zz, yy, kk):
        return zz * 8 + lax.rem(yy + 4, 4) * 2 + kk

    def remote(src, dst, send, recv, dev):
        return pltpu.make_async_remote_copy(
            src_ref=src, dst_ref=dst, send_sem=send, recv_sem=recv, device_id=dev, device_id_type=MESH
        )

    me = ctx_dev(lax.rem(ctx + 1, 16))

    def wait_recv(ref, send, recv):
        remote(ref, ref, send, recv, me).wait_recv()

    def wait_send(ref, send, recv):
        remote(ref, ref, send, recv, me).wait_send()

    def cols(i):
        return pl.ds(pl.multiple_of(i * PIECE, PIECE), PIECE)

    def rows(i, n):
        return pl.ds(pl.multiple_of(i * n, n), n)

    local_k = pltpu.make_async_copy(k_in, kv.at[0], lsem.at[0])
    local_v = pltpu.make_async_copy(v_in, kv.at[1], lsem.at[1])
    local_k.start()
    local_v.start()
    local_w = pltpu.make_async_copy(w_in, wrows.at[zh, :, cols(x)], lsem.at[5])
    local_h = pltpu.make_async_copy(h_in, taps.at[rows(dp, ROWS), :], lsem.at[6])
    local_h.start()
    local_w.start()
    local_q = pltpu.make_async_copy(q_in.at[:, cols(ctx)], qc.at[rows(ctx, ROWS), :], lsem.at[7])
    local_q.start()
    for part in range(PARTS):
        for xx in range(4):
            pltpu.make_async_copy(
                og_in.at[:, pl.ds((xx * 4 + part) * PIECE, PIECE)],
                cot.at[part, rows(ctx, ROWS), pl.ds(xx * PIECE, PIECE)],
                lsem.at[4],
            ).start()
    local_fwd = pltpu.make_async_copy(fwd_in, fwd, lsem.at[2])
    local_inv = pltpu.make_async_copy(inv_in, inv, lsem.at[3])
    local_fwd.start()
    local_inv.start()

    barrier = pltpu.get_barrier_semaphore()

    def greet(off, carry):
        pl.semaphore_signal(barrier, inc=1, device_id=ctx_dev(lax.rem(ctx + off, 16)), device_id_type=MESH)
        return carry

    lax.fori_loop(1, 16, greet, 0)
    for off in range(1, 4):
        pl.semaphore_signal(barrier, inc=1, device_id=dp_dev(lax.rem(x + off, 4), zh), device_id_type=MESH)
        pl.semaphore_signal(barrier, inc=1, device_id=dp_dev(x, lax.rem(zh + off, 4)), device_id_type=MESH)
    pl.semaphore_wait(barrier, 21)

    local_h.wait()
    local_w.wait()
    for off in range(1, 4):
        dev = dp_dev(x, lax.rem(zh + off, 4))
        own = taps.at[rows(dp, ROWS), :]
        remote(own, own, ss_par.at[0], rs_par.at[0], dev).start()

    def send_q(off, carry):
        c = lax.rem(ctx + off, 16)
        remote(q_in.at[:, cols(c)], qc.at[rows(ctx, ROWS), :], ss_in.at[0], rs_in.at[0], ctx_dev(c)).start()
        return carry

    lax.fori_loop(1, 16, send_q, 0)
    for off in range(1, 4):
        dev = dp_dev(x, lax.rem(zh + off, 4))
        own = wrows.at[zh, :, cols(x)]
        remote(own, own, ss_par.at[1], rs_par.at[1], dev).start()

    local_k.wait()
    local_v.wait()

    def product(i, carry):
        piece = cols(i)
        ub[:, piece] = (kv[0, :, piece].astype(F32) * kv[1, :, piece].astype(F32)).astype(BF16)
        return carry

    lax.fori_loop(0, 16, product, 0)
    local_u = pltpu.make_async_copy(ub.at[:, cols(ctx)], uc.at[rows(ctx, ROWS), :], lsem.at[8])
    local_u.start()

    def send_u(off, carry):
        c = lax.rem(ctx + off, 16)
        remote(ub.at[:, cols(c)], uc.at[rows(ctx, ROWS), :], ss_in.at[1], rs_in.at[1], ctx_dev(c)).start()
        return carry

    lax.fori_loop(1, 16, send_u, 0)

    dev_z = ctx_dev(ctx_of(1 - zl, y, core))
    dev_up = ctx_dev(ctx_of(zl, y + 1, core))
    dev_down = ctx_dev(ctx_of(zl, y - 1, core))
    dev_sib = ctx_dev(ctx_of(zl, y, 1 - core))

    def spread(part, c, start, count, recv, dev):
        piece = cot.at[part, pl.ds(pl.multiple_of(c * ROWS + start, 64), count), :]
        remote(piece, piece, ss_ag.at[part], recv.at[part], dev).start()

    def arrived(part, count, recv):
        wait_recv(cot.at[part, pl.ds(0, count), :], ss_ag.at[part], recv.at[part])

    def gather_own(part):
        spread(part, ctx, 0, ROWS, rs_z, dev_z)
        spread(part, ctx, 0, ROWS, rs_ym, dev_up)
        spread(part, ctx, 0, ROWS, rs_yp, dev_down)
        spread(part, ctx, 0, ROWS, rs_sib, dev_sib)

    def gather_pair(part):
        arrived(part, ROWS, rs_z)
        c = ctx_of(1 - zl, y, core)
        spread(part, c, 0, ROWS, rs_zym, dev_up)
        spread(part, c, 0, ROWS, rs_zyp, dev_down)
        spread(part, c, 0, ROWS, rs_sib, dev_sib)

    def gather_near(part, zz, from_down, from_up):
        arrived(part, ROWS, from_down)
        c = ctx_of(zz, y - 1, core)
        spread(part, c, 0, 64, rs_far, dev_up)
        spread(part, c, 0, ROWS, rs_sib, dev_sib)
        arrived(part, ROWS, from_up)
        c = ctx_of(zz, y + 1, core)
        spread(part, c, 64, 64, rs_far, dev_down)
        spread(part, c, 0, ROWS, rs_sib, dev_sib)

    def gather_far(part):
        arrived(part, 2 * ROWS, rs_far)
        spread(part, ctx_of(zl, y + 2, core), 0, ROWS, rs_sib, dev_sib)
        spread(part, ctx_of(1 - zl, y + 2, core), 0, ROWS, rs_sib, dev_sib)

    pltpu.make_async_copy(cot.at[0, pl.ds(0, 512), :], cot.at[0, pl.ds(0, 512), :], lsem.at[4]).wait()
    gather_own(0)
    gather_own(1)

    wait_recv(taps.at[pl.ds(0, 3 * ROWS), :], ss_par.at[0], rs_par.at[0])
    for off in range(1, 4):
        own = taps.at[rows(x, BLOCK), :]
        remote(own, own, ss_par.at[2], rs_par.at[2], dp_dev(lax.rem(x + off, 4), zh)).start()
    wait_recv(wrows.at[0, pl.ds(0, 192), :], ss_par.at[1], rs_par.at[1])
    for off in range(1, 4):
        own = wrows.at[:, :, cols(x)]
        remote(own, own, ss_par.at[3], rs_par.at[3], dp_dev(lax.rem(x + off, 4), zh)).start()

    def forward(source, spec):
        def step(i, carry):
            spec[i] = jnp.dot(fwd[...], source[rows(i, BLOCK), :], preferred_element_type=F32)
            return carry

        lax.fori_loop(0, 4, step, 0)

    def over_tiles(body):
        for half in range(2):
            sign = 1.0 - 2.0 * half

            def step(i, carry):
                base = pl.multiple_of(half * 256 + i * 16, 16)
                for lane in range(2):
                    body(pl.ds(base, 16), pl.ds(base + BLOCK, 16), pl.ds(lane * 128, 128), sign)
                return carry

            lax.fori_loop(0, 16, step, 0)

    local_fwd.wait()
    local_inv.wait()
    wait_recv(taps.at[pl.ds(0, 3 * BLOCK), :], ss_par.at[2], rs_par.at[2])
    forward(taps, spec_g)

    def window(re, im, lane, sign):
        for d in (3, 2, 1):
            real = spec_g[d, re, lane] - sign * spec_g[d - 1, im, lane]
            imag = spec_g[d, im, lane] + sign * spec_g[d - 1, re, lane]
            spec_g[d, re, lane] = real
            spec_g[d, im, lane] = imag

    over_tiles(window)

    local_u.wait()
    wait_recv(uc.at[pl.ds(0, 15 * ROWS), :], ss_in.at[1], rs_in.at[1])
    forward(uc, spec_u)
    gather_pair(0)

    def convolve(re, im, lane, sign):
        ure = [spec_u[a, re, lane] for a in range(4)]
        uim = [spec_u[a, im, lane] for a in range(4)]
        gre = [spec_g[a, re, lane] for a in range(4)]
        gim = [spec_g[a, im, lane] for a in range(4)]
        for i in range(4):
            prod[i, re, lane] = sum(ure[a] * gre[i - a] - uim[a] * gim[i - a] for a in range(i + 1)).astype(BF16)
            prod[i, im, lane] = sum(ure[a] * gim[i - a] + uim[a] * gre[i - a] for a in range(i + 1)).astype(BF16)

    over_tiles(convolve)
    local_q.wait()
    wait_recv(qc.at[pl.ds(0, 15 * ROWS), :], ss_in.at[0], rs_in.at[0])

    def conv_out(i, carry):
        out = jnp.dot(inv[...], prod[i], preferred_element_type=F32)
        zbuf[rows(i, BLOCK), :] = out
        return carry

    lax.fori_loop(0, 4, conv_out, 0)
    gather_near(0, zl, rs_ym, rs_yp)

    def gate(i, carry):
        block = rows(i, 256)
        gated = (qc[block, :].astype(F32) * zbuf[block, :]).astype(BF16).astype(F32)
        gtr[:, block] = gated.T.astype(BF16)
        dgbuf[block, :] = jnp.zeros((256, CHAN), F32)
        return carry

    lax.fori_loop(0, 8, gate, 0)
    wait_recv(wrows.at[pl.ds(0, 3)], ss_par.at[3], rs_par.at[3])

    def reduce_far(part):
        wait_recv(wrecv.at[part, pl.ds(0, 3)], ss_w.at[part], rs_w.at[part])
        total = wown[part]
        for off in range(1, 4):
            total = total + wrecv[part, lax.rem(x + off, 4)].astype(F32)

        @pl.when(zh == part)
        def _():
            wfin[...] = total

        @pl.when(zh != part)
        def _():
            wsend2[part] = total.astype(BF16)
            remote(wsend2.at[part], wrecv2.at[zh], ss_w2.at[0], rs_w2.at[0], dp_dev(x, part)).start()

    def slab(part, carry):
        gather_near(part, 1 - zl, rs_zym, rs_zyp)

        @pl.when(part < 3)
        def _():
            gather_pair(part + 1)

        @pl.when(part < 2)
        def _():
            gather_own(part + 2)

        gather_far(part)

        @pl.when(part < 3)
        def _():
            gather_near(part + 1, zl, rs_ym, rs_yp)

        arrived(part, 8 * ROWS, rs_sib)

        def grad_gated(i, carry):
            block = rows(i, BLOCK)
            dgbuf[block, :] += lax.dot_general(
                cot[part, block, :], wrows[part], (((1,), (1,)), ((), ())), preferred_element_type=F32
            )
            return carry

        def weight_term(i, carry):
            term = jnp.dot(gtr[...], cot[part, :, cols(i)], preferred_element_type=F32)
            wsend[part, i] = term.astype(BF16)

            @pl.when(i == x)
            def _():
                wown[part] = term

            return carry

        lax.fori_loop(0, 4, weight_term, 0)
        for off in range(1, 4):
            xx = lax.rem(x + off, 4)
            remote(wsend.at[part, xx], wrecv.at[part, x], ss_w.at[part], rs_w.at[part], dp_dev(xx, zh)).start()
        lax.fori_loop(0, 4, grad_gated, 0)

        @pl.when(part > 0)
        def _():
            reduce_far(part - 1)

        return carry

    lax.fori_loop(0, PARTS, slab, 0)

    def finish_dg(i, carry):
        block = rows(i, ROWS)
        grad = dgbuf[block, :]
        qgc[block, :] = (grad * zbuf[block, :]).astype(BF16)
        dzb[block, :] = (grad * qc[block, :].astype(F32)).astype(BF16)
        return carry

    lax.fori_loop(0, 16, finish_dg, 0)

    def send_back(source, target, index):
        own = pltpu.make_async_copy(source.at[rows(ctx, ROWS), :], target.at[:, cols(ctx)], lsem.at[9 + index])
        own.start()

        def step(off, carry):
            c = lax.rem(ctx + off, 16)
            remote(
                source.at[rows(c, ROWS), :], target.at[:, cols(ctx)], ss_out.at[index], rs_out.at[index], ctx_dev(c)
            ).start()
            return carry

        lax.fori_loop(1, 16, step, 0)
        return own

    own_qg = send_back(qgc, qg_out, 0)
    forward(dzb, spec_d)

    def correlate(re, im, lane, sign):
        gre = [spec_g[a, re, lane] for a in range(4)]
        gim = [spec_g[a, im, lane] for a in range(4)]
        dre = [spec_d[a, re, lane] for a in range(4)]
        dim = [spec_d[a, im, lane] for a in range(4)]
        for a in range(4):
            prod[a, re, lane] = sum(gre[i - a] * dre[i] + gim[i - a] * dim[i] for i in range(a, 4)).astype(BF16)
            prod[a, im, lane] = sum(gre[i - a] * dim[i] - gim[i - a] * dre[i] for i in range(a, 4)).astype(BF16)

    over_tiles(correlate)

    def grad_prod(i, carry):
        duc[rows(i, BLOCK), :] = jnp.dot(inv[...], prod[i], preferred_element_type=F32).astype(BF16)
        return carry

    lax.fori_loop(0, 4, grad_prod, 0)
    own_du = send_back(duc, du_out, 1)
    reduce_far(3)

    def filter_product(re, im, lane, sign):
        ure = [spec_u[a, re, lane] for a in range(4)]
        uim = [spec_u[a, im, lane] for a in range(4)]
        dre = [spec_d[a, re, lane] for a in range(4)]
        dim = [spec_d[a, im, lane] for a in range(4)]
        after = None
        for d in (3, 2, 1, 0):
            real = sum(ure[a] * dre[a + d] + uim[a] * dim[a + d] for a in range(4 - d))
            imag = sum(ure[a] * dim[a + d] - uim[a] * dre[a + d] for a in range(4 - d))
            if after is None:
                prod[d, re, lane] = real.astype(BF16)
                prod[d, im, lane] = imag.astype(BF16)
            else:
                prod[d, re, lane] = (real + sign * after[1]).astype(BF16)
                prod[d, im, lane] = (imag - sign * after[0]).astype(BF16)
            after = (real, imag)

    over_tiles(filter_product)

    def filter_term(i, carry):
        term = jnp.dot(inv[...], prod[i], preferred_element_type=F32)
        fsend[i] = term.astype(BF16)

        @pl.when(i == x)
        def _():
            fown[...] = term

        return carry

    lax.fori_loop(0, 4, filter_term, 0)
    for off in range(1, 4):
        xx = lax.rem(x + off, 4)
        remote(fsend.at[xx], frecv.at[x], ss_f.at[0], rs_f.at[0], dp_dev(xx, zh)).start()
    wait_recv(frecv.at[pl.ds(0, 3)], ss_f.at[0], rs_f.at[0])
    for off in range(1, 4):
        fown[...] += frecv[lax.rem(x + off, 4)].astype(F32)
    for off in range(1, 4):
        zz = lax.rem(zh + off, 4)
        fsend2[zz] = fown[rows(zz, ROWS), :].astype(BF16)
        remote(fsend2.at[zz], frecv2.at[zh], ss_f.at[1], rs_f.at[1], dp_dev(x, zz)).start()

    wait_recv(wrecv2.at[pl.ds(0, 3)], ss_w2.at[0], rs_w2.at[0])
    weight = wfin[...]
    for off in range(1, 4):
        weight = weight + wrecv2[lax.rem(zh + off, 4)].astype(F32)
    wg_out[...] = weight * (1.0 / 16.0)
    wait_recv(frecv2.at[pl.ds(0, 3)], ss_f.at[1], rs_f.at[1])
    grad = fown[rows(zh, ROWS), :]
    for off in range(1, 4):
        grad = grad + frecv2[lax.rem(zh + off, 4)].astype(F32)
    fg_out[...] = grad * (1.0 / 16.0)

    own_qg.wait()
    own_du.wait()
    for index in range(2):
        wait_send(uc.at[pl.ds(0, 15 * ROWS), :], ss_in.at[index], rs_in.at[index])
        wait_send(qgc.at[pl.ds(0, 15 * ROWS), :], ss_out.at[index], rs_out.at[index])
        wait_recv(qgc.at[pl.ds(0, 15 * ROWS), :], ss_out.at[index], rs_out.at[index])
    wait_send(taps.at[pl.ds(0, 3 * ROWS), :], ss_par.at[0], rs_par.at[0])
    wait_send(wrows.at[0, pl.ds(0, 192), :], ss_par.at[1], rs_par.at[1])
    wait_send(taps.at[pl.ds(0, 3 * BLOCK), :], ss_par.at[2], rs_par.at[2])
    wait_send(wrows.at[pl.ds(0, 3)], ss_par.at[3], rs_par.at[3])

    def drain(part, carry):
        wait_send(cot.at[part, pl.ds(0, 15 * ROWS), :], ss_ag.at[part], rs_z.at[part])
        wait_send(wsend.at[part, pl.ds(0, 3)], ss_w.at[part], rs_w.at[part])
        return carry

    lax.fori_loop(0, PARTS, drain, 0)
    wait_send(wsend2.at[pl.ds(0, 3)], ss_w2.at[0], rs_w2.at[0])
    wait_send(fsend.at[pl.ds(0, 3)], ss_f.at[0], rs_f.at[0])
    wait_send(fsend2.at[pl.ds(0, 3)], ss_f.at[1], rs_f.at[1])


def shards(query_act, key_act, value_act, out_grad, out_weight, filter_taps):
    fwd, inv = transform_tables()
    anywhere = pl.BlockSpec(memory_space=pl.ANY)
    inside = pl.BlockSpec(memory_space=pltpu.VMEM)
    dma = pltpu.SemaphoreType.DMA

    def vmem(shape, dtype):
        return pltpu.VMEM(shape, dtype)

    query_grad, grad_prod, weight_grad, filter_grad = pl.pallas_call(
        kernel,
        out_shape=(
            jax.ShapeDtypeStruct((ROWS, WIDTH), BF16),
            jax.ShapeDtypeStruct((ROWS, WIDTH), BF16),
            jax.ShapeDtypeStruct((CHAN, PIECE), F32),
            jax.ShapeDtypeStruct((ROWS, CHAN), F32),
        ),
        in_specs=[anywhere] * 8,
        out_specs=(anywhere, anywhere, inside, inside),
        scratch_shapes=[
            vmem((2, ROWS, WIDTH), BF16),
            vmem((ROWS, WIDTH), BF16),
            vmem((2 * BLOCK, BLOCK), BF16),
            vmem((BLOCK, 2 * BLOCK), BF16),
            vmem((PARTS, SEQ, SLAB), BF16),
            vmem((PARTS, CHAN, SLAB), BF16),
            vmem((SEQ, CHAN), BF16),
            vmem((SEQ, CHAN), BF16),
            vmem((SEQ, CHAN), BF16),
            vmem((4, 2 * BLOCK, CHAN), F32),
            vmem((4, 2 * BLOCK, CHAN), F32),
            vmem((4, 2 * BLOCK, CHAN), F32),
            vmem((4, 2 * BLOCK, CHAN), BF16),
            vmem((SEQ, CHAN), F32),
            vmem((SEQ, CHAN), F32),
            vmem((CHAN, SEQ), BF16),
            vmem((SEQ, CHAN), BF16),
            vmem((SEQ, CHAN), BF16),
            vmem((SEQ, CHAN), BF16),
            vmem((PARTS, 4, CHAN, PIECE), BF16),
            vmem((PARTS, 4, CHAN, PIECE), BF16),
            vmem((PARTS, CHAN, PIECE), F32),
            vmem((PARTS, CHAN, PIECE), BF16),
            vmem((4, CHAN, PIECE), BF16),
            vmem((CHAN, PIECE), F32),
            vmem((4, BLOCK, CHAN), BF16),
            vmem((4, BLOCK, CHAN), BF16),
            vmem((BLOCK, CHAN), F32),
            vmem((4, ROWS, CHAN), BF16),
            vmem((4, ROWS, CHAN), BF16),
            dma((11,)),
            dma((2,)), dma((2,)),
            dma((4,)), dma((4,)),
            dma((PARTS,)),
            dma((PARTS,)), dma((PARTS,)), dma((PARTS,)), dma((PARTS,)), dma((PARTS,)), dma((PARTS,)), dma((PARTS,)),
            dma((PARTS,)), dma((PARTS,)),
            dma((1,)), dma((1,)),
            dma((2,)), dma((2,)),
            dma((2,)), dma((2,)),
        ],
        compiler_params=pltpu.CompilerParams(
            collective_id=0, has_side_effects=True, vmem_limit_bytes=60 * 1024 * 1024
        ),
        cost_estimate=pl.CostEstimate(flops=16_000_000_000, bytes_accessed=16_000_000, transcendentals=0),
        name="hyena_backward",
    )(query_act, key_act, value_act, out_grad, out_weight, filter_taps, fwd, inv)
    spread = grad_prod.astype(F32)
    key_grad = (spread * value_act.astype(F32)).astype(BF16)
    value_grad = (spread * key_act.astype(F32)).astype(BF16)
    return query_grad, key_grad, value_grad, weight_grad, filter_grad


def solution(mesh):
    return jax.shard_map(
        shards,
        mesh=mesh,
        in_specs=(
            P(("dp", "context"), None),
            P(("dp", "context"), None),
            P(("dp", "context"), None),
            P(("dp", "context"), None),
            P("context", "dp"),
            P("dp", "context"),
        ),
        out_specs=(
            P(("dp", "context"), None),
            P(("dp", "context"), None),
            P(("dp", "context"), None),
            P("context", "dp"),
            P("dp", "context"),
        ),
        check_vma=False,
    )
```

```python
import math

import jax
import jax.numpy as jnp
import numpy as np
from jax import lax
from jax.experimental import pallas as pl
from jax.experimental.pallas import tpu as pltpu
from jax.sharding import PartitionSpec as P

SEQ = 2048
CHAN = 256
ROWS = 128
WIDTH = 4096
BLOCK = 512
PARTS = 4
SLAB = 1024
PIECE = 256
FAR_BY_PAIR = (0, 1, 2, 3)
F32 = jnp.float32
BF16 = jnp.bfloat16
MESH = pl.DeviceIdType.MESH


def transform_tables():
    freq = np.concatenate([np.arange(0, BLOCK, 2), np.arange(1, BLOCK, 2)])
    time = np.arange(BLOCK)
    angle = ((2 * freq[:, None] + 1) * time[None, :] % (4 * BLOCK)) * (math.pi / (2 * BLOCK))
    table = np.concatenate([np.cos(angle), -np.sin(angle)], axis=0)
    return jnp.asarray(table, BF16), jnp.asarray(table.T / BLOCK, BF16)


def kernel(
    q_in, k_in, v_in, og_in, w_in, h_in, fwd_in, inv_in,
    qg_out, du_out, wg_out, fg_out,
    kv, ub, fwd, inv, cot, wrows, taps, qc, uc, spec_u, spec_g, spec_d, prod, zbuf, dgbuf, gtr, dzb, qgc, duc,
    wsend, wrecv, wown, wsend2, wrecv2, wrelay, fsend, frecv, fown, fsend2, frecv2, frelay,
    lsem, ss_in, rs_in, ss_par, rs_par, ss_ag, rs_z, rs_ym, rs_yp, rs_zym, rs_zyp, rs_far, rs_sib, rs_zfar, rs_zsib,
    ss_w, rs_w, ss_w2, rs_w2, rs_relay, ss_f, rs_f, ss_out, rs_out,
):
    dp = lax.axis_index("dp")
    ctx = lax.axis_index("context")
    x, zh = dp // 4, dp % 4
    zl, y, core = ctx // 8, (ctx // 2) % 4, ctx % 2

    def ctx_dev(c):
        return {"dp": dp, "context": c}

    def dp_dev(xx, zz):
        return {"dp": xx * 4 + zz, "context": ctx}

    def ctx_of(zz, yy, kk):
        return zz * 8 + lax.rem(yy + 4, 4) * 2 + kk

    def remote(src, dst, send, recv, dev):
        return pltpu.make_async_remote_copy(
            src_ref=src, dst_ref=dst, send_sem=send, recv_sem=recv, device_id=dev, device_id_type=MESH
        )

    me = ctx_dev(lax.rem(ctx + 1, 16))

    def wait_recv(ref, send, recv):
        remote(ref, ref, send, recv, me).wait_recv()

    def wait_send(ref, send, recv):
        remote(ref, ref, send, recv, me).wait_send()

    def cols(i):
        return pl.ds(pl.multiple_of(i * PIECE, PIECE), PIECE)

    def rows(i, n):
        return pl.ds(pl.multiple_of(i * n, n), n)

    local_k = pltpu.make_async_copy(k_in, kv.at[0], lsem.at[0])
    local_v = pltpu.make_async_copy(v_in, kv.at[1], lsem.at[1])
    local_k.start()
    local_v.start()
    local_w = pltpu.make_async_copy(w_in, wrows.at[zh, :, cols(x)], lsem.at[5])
    local_h = pltpu.make_async_copy(h_in, taps.at[rows(dp, ROWS), :], lsem.at[6])
    local_h.start()
    local_w.start()
    local_q = pltpu.make_async_copy(q_in.at[:, cols(ctx)], qc.at[rows(ctx, ROWS), :], lsem.at[7])
    local_q.start()
    for part in range(PARTS):
        for xx in range(4):
            pltpu.make_async_copy(
                og_in.at[:, pl.ds((xx * 4 + part) * PIECE, PIECE)],
                cot.at[part, rows(ctx, ROWS), pl.ds(xx * PIECE, PIECE)],
                lsem.at[4],
            ).start()
    local_fwd = pltpu.make_async_copy(fwd_in, fwd, lsem.at[2])
    local_inv = pltpu.make_async_copy(inv_in, inv, lsem.at[3])
    local_fwd.start()
    local_inv.start()

    barrier = pltpu.get_barrier_semaphore()

    def greet(off, carry):
        pl.semaphore_signal(barrier, inc=1, device_id=ctx_dev(lax.rem(ctx + off, 16)), device_id_type=MESH)
        return carry

    lax.fori_loop(1, 16, greet, 0)
    for off in range(1, 4):
        pl.semaphore_signal(barrier, inc=1, device_id=dp_dev(lax.rem(x + off, 4), zh), device_id_type=MESH)
        pl.semaphore_signal(barrier, inc=1, device_id=dp_dev(x, lax.rem(zh + off, 4)), device_id_type=MESH)
    pl.semaphore_wait(barrier, 21)

    local_h.wait()
    z_up = dp_dev(x, lax.rem(zh + 1, 4))
    z_down = dp_dev(x, lax.rem(zh + 3, 4))

    def send_taps(zz, start, count, index, dev):
        piece = taps.at[pl.ds(pl.multiple_of((x * 4 + zz) * ROWS + start, 64), count), :]
        remote(piece, piece, ss_par.at[0], rs_par.at[index], dev).start()

    def send_rows(zz, start, count, index, dev):
        piece = wrows.at[zz, pl.ds(start, count), cols(x)]
        remote(piece, piece, ss_par.at[1], rs_par.at[index], dev).start()

    send_taps(zh, 0, ROWS, 0, z_up)
    send_taps(zh, 0, ROWS, 1, z_down)

    local_w.wait()
    send_rows(zh, 0, CHAN, 3, z_up)
    send_rows(zh, 0, CHAN, 4, z_down)

    local_k.wait()
    local_v.wait()

    def product(i, carry):
        piece = cols(i)
        ub[:, piece] = (kv[0, :, piece].astype(F32) * kv[1, :, piece].astype(F32)).astype(BF16)
        return carry

    lax.fori_loop(0, 16, product, 0)
    local_u = pltpu.make_async_copy(ub.at[:, cols(ctx)], uc.at[rows(ctx, ROWS), :], lsem.at[8])
    local_u.start()

    dev_z = ctx_dev(ctx_of(1 - zl, y, core))
    dev_up = ctx_dev(ctx_of(zl, y + 1, core))
    dev_down = ctx_dev(ctx_of(zl, y - 1, core))
    dev_sib = ctx_dev(ctx_of(zl, y, 1 - core))

    def spread(part, c, start, count, recv, dev):
        piece = cot.at[part, pl.ds(pl.multiple_of(c * ROWS + start, 64), count), :]
        remote(piece, piece, ss_ag.at[part], recv.at[part], dev).start()

    def arrived(part, count, recv):
        wait_recv(cot.at[part, pl.ds(0, count), :], ss_ag.at[part], recv.at[part])

    def gather_own_z(part):
        spread(part, ctx, 0, ROWS, rs_z, dev_z)

    def gather_own_y(part):
        spread(part, ctx, 0, ROWS, rs_ym, dev_up)
        spread(part, ctx, 0, ROWS, rs_yp, dev_down)
        spread(part, ctx, 0, ROWS, rs_sib, dev_sib)

    def gather_pair(part):
        arrived(part, ROWS, rs_z)
        c = ctx_of(1 - zl, y, core)
        spread(part, c, 0, ROWS, rs_zym, dev_up)
        spread(part, c, 0, ROWS, rs_zyp, dev_down)
        spread(part, c, 0, ROWS, rs_zsib, dev_sib)

    def gather_near(part, own):
        zz = zl if own else 1 - zl
        from_down, from_up = (rs_ym, rs_yp) if own else (rs_zym, rs_zyp)
        far, sib = (rs_far, rs_sib) if own else (rs_zfar, rs_zsib)
        halves = own or part not in FAR_BY_PAIR
        arrived(part, ROWS, from_down)
        c = ctx_of(zz, y - 1, core)
        if halves:
            spread(part, c, 0, 64, far, dev_up)
        spread(part, c, 0, ROWS, sib, dev_sib)
        arrived(part, ROWS, from_up)
        c = ctx_of(zz, y + 1, core)
        if halves:
            spread(part, c, 64, 64, far, dev_down)
        spread(part, c, 0, ROWS, sib, dev_sib)

    def gather_far(part, own):
        zz = zl if own else 1 - zl
        far, sib = (rs_far, rs_sib) if own else (rs_zfar, rs_zsib)
        arrived(part, ROWS, far)
        c = ctx_of(zz, y + 2, core)
        if own and part in FAR_BY_PAIR:
            spread(part, c, 0, ROWS, rs_zfar, dev_z)
        spread(part, c, 0, ROWS, sib, dev_sib)

    def complete(part, own):
        arrived(part, 4 * ROWS, rs_sib if own else rs_zsib)

    pltpu.make_async_copy(cot.at[0, pl.ds(0, 512), :], cot.at[0, pl.ds(0, 512), :], lsem.at[4]).wait()
    gather_own_y(0)
    gather_own_y(1)
    gather_own_y(2)
    for start, recv, dev, away in ((0, 0, z_up, 3), (64, 1, z_down, 1)):
        wait_recv(taps.at[pl.ds(0, ROWS), :], ss_par.at[0], rs_par.at[recv])
        send_taps(lax.rem(zh + away, 4), start, 64, 2, dev)
    for start, recv, dev, away in ((0, 3, z_up, 3), (128, 4, z_down, 1)):
        wait_recv(wrows.at[0, pl.ds(0, 64), :], ss_par.at[1], rs_par.at[recv])
        send_rows(lax.rem(zh + away, 4), start, 128, 5, dev)

    def send_u(off, carry):
        c = lax.rem(ctx + off, 16)
        remote(ub.at[:, cols(c)], uc.at[rows(ctx, ROWS), :], ss_in.at[1], rs_in.at[1], ctx_dev(c)).start()
        return carry

    lax.fori_loop(1, 16, send_u, 0)

    def send_q(off, carry):
        c = lax.rem(ctx + off, 16)
        remote(q_in.at[:, cols(c)], qc.at[rows(ctx, ROWS), :], ss_in.at[0], rs_in.at[0], ctx_dev(c)).start()
        return carry

    lax.fori_loop(1, 16, send_q, 0)

    gather_own_z(0)
    gather_own_z(1)
    gather_own_z(2)
    gather_own_z(3)
    gather_near(0, True)

    wait_recv(taps.at[pl.ds(0, ROWS), :], ss_par.at[0], rs_par.at[2])
    for off in range(1, 4):
        own = taps.at[rows(x, BLOCK), :]
        remote(own, own, ss_par.at[2], rs_par.at[6], dp_dev(lax.rem(x + off, 4), zh)).start()
    wait_recv(wrows.at[0, pl.ds(0, 64), :], ss_par.at[1], rs_par.at[5])
    for off in range(1, 4):
        own = wrows.at[:, :, cols(x)]
        remote(own, own, ss_par.at[3], rs_par.at[7], dp_dev(lax.rem(x + off, 4), zh)).start()
    gather_own_y(3)
    gather_near(1, True)
    gather_near(2, True)

    def forward(source, spec, first, count):
        def step(j, carry):
            i = first + j
            spec[i] = jnp.dot(fwd[...], source[rows(i, BLOCK), :], preferred_element_type=F32)
            return carry

        lax.fori_loop(0, count, step, 0)

    def over_tiles(body):
        for half in range(2):
            sign = 1.0 - 2.0 * half

            def step(i, carry):
                base = pl.multiple_of(half * 256 + i * 16, 16)
                for lane in range(2):
                    body(pl.ds(base, 16), pl.ds(base + BLOCK, 16), pl.ds(lane * 128, 128), sign)
                return carry

            lax.fori_loop(0, 16, step, 0)

    local_fwd.wait()
    local_inv.wait()
    wait_recv(taps.at[pl.ds(0, 3 * BLOCK), :], ss_par.at[2], rs_par.at[6])
    forward(taps, spec_g, 0, 4)

    def window(re, im, lane, sign):
        for d in (3, 2, 1):
            real = spec_g[d, re, lane] - sign * spec_g[d - 1, im, lane]
            imag = spec_g[d, im, lane] + sign * spec_g[d - 1, re, lane]
            spec_g[d, re, lane] = real
            spec_g[d, im, lane] = imag

    over_tiles(window)

    local_u.wait()
    wait_recv(uc.at[pl.ds(0, 15 * ROWS), :], ss_in.at[1], rs_in.at[1])
    forward(uc, spec_u, 0, 4)

    def convolve(re, im, lane, sign):
        ure = [spec_u[a, re, lane] for a in range(4)]
        uim = [spec_u[a, im, lane] for a in range(4)]
        gre = [spec_g[a, re, lane] for a in range(4)]
        gim = [spec_g[a, im, lane] for a in range(4)]
        for i in range(4):
            prod[i, re, lane] = sum(ure[a] * gre[i - a] - uim[a] * gim[i - a] for a in range(i + 1)).astype(BF16)
            prod[i, im, lane] = sum(ure[a] * gim[i - a] + uim[a] * gre[i - a] for a in range(i + 1)).astype(BF16)

    over_tiles(convolve)
    local_q.wait()
    wait_recv(qc.at[pl.ds(0, 15 * ROWS), :], ss_in.at[0], rs_in.at[0])

    def conv_out(i, carry):
        out = jnp.dot(inv[...], prod[i], preferred_element_type=F32)
        zbuf[rows(i, BLOCK), :] = out
        return carry

    lax.fori_loop(0, 4, conv_out, 0)

    def gate(i, carry):
        block = rows(i, 256)
        gated = (qc[block, :].astype(F32) * zbuf[block, :]).astype(BF16).astype(F32)
        gtr[:, block] = gated.T.astype(BF16)
        dgbuf[block, :] = jnp.zeros((256, CHAN), F32)
        return carry

    lax.fori_loop(0, 8, gate, 0)
    def reduce_near(part):
        wait_recv(wrecv.at[part, pl.ds(0, 3)], ss_w.at[part], rs_w.at[part])
        total = wown[part]
        for off in range(1, 4):
            total = total + wrecv[part, lax.rem(x + off, 4)].astype(F32)
        wown[part] = total

        @pl.when(lax.rem(zh + 2, 4) == part)
        def _():
            wsend2[part] = total.astype(BF16)
            for start, dev in ((0, z_up), (128, z_down)):
                half = pl.ds(start, 128)
                remote(
                    wsend2.at[part, half, :], wrelay.at[part, half, :], ss_w2.at[0], rs_relay.at[part], dev
                ).start()

    def reduce_far(part):
        for away, start, dev in ((1, 0, z_up), (3, 128, z_down)):
            half = pl.ds(start, 128)

            @pl.when(lax.rem(zh + away, 4) == part)
            def _():
                wait_recv(wrelay.at[part, half, :], ss_w2.at[0], rs_relay.at[part])
                wown[part, half, :] += wrelay[part, half, :].astype(F32)
                wsend2[part] = wown[part].astype(BF16)
                remote(wsend2.at[part], wrecv2.at[away // 2], ss_w2.at[0], rs_w2.at[0], dev).start()

    def weight_term(part):
        def product_of(xx):
            return jnp.dot(gtr[...], cot[part, :, cols(xx)], preferred_element_type=F32)

        def step(off, carry):
            xx = lax.rem(x + off, 4)
            wsend[part, xx] = product_of(xx).astype(BF16)
            remote(wsend.at[part, xx], wrecv.at[part, x], ss_w.at[part], rs_w.at[part], dp_dev(xx, zh)).start()
            return carry

        lax.fori_loop(1, 4, step, 0)
        wown[part] = product_of(x)

    def grad_gated(part, own):
        zz = zl if own else 1 - zl

        def step(i, carry):
            block = rows(zz * 2 + i, BLOCK)
            dgbuf[block, :] += lax.dot_general(
                cot[part, block, :], wrows[part], (((1,), (1,)), ((), ())), preferred_element_type=F32
            )
            return carry

        lax.fori_loop(0, 2, step, 0)

    def send_back(source, target, index, c):
        @pl.when(c != ctx)
        def _():
            remote(
                source.at[rows(c, ROWS), :], target.at[:, cols(ctx)], ss_out.at[index], rs_out.at[index], ctx_dev(c)
            ).start()

    def keep_back(source, target, index):
        return pltpu.make_async_copy(source.at[rows(ctx, ROWS), :], target.at[:, cols(ctx)], lsem.at[9 + index])

    def finish_dg(own):
        zz = zl if own else 1 - zl

        def step(off, carry):
            c = zz * 8 + lax.rem(ctx + off, 8)
            block = rows(c, ROWS)
            grad = dgbuf[block, :]
            qgc[block, :] = (grad * zbuf[block, :]).astype(BF16)
            dzb[block, :] = (grad * qc[block, :].astype(F32)).astype(BF16)
            send_back(qgc, qg_out, 0, c)
            return carry

        lax.fori_loop(0, 8, step, 0)
        forward(dzb, spec_d, zz * 2, 2)

    gather_pair(0)
    gather_near(3, True)
    gather_far(0, True)
    gather_pair(1)
    gather_far(1, True)
    gather_far(2, True)
    gather_pair(2)
    wait_recv(wrows.at[pl.ds(0, 3)], ss_par.at[3], rs_par.at[7])
    complete(0, True)
    grad_gated(0, True)
    gather_pair(3)
    complete(1, True)
    grad_gated(1, True)
    gather_far(3, True)
    complete(2, True)
    grad_gated(2, True)
    complete(3, True)
    grad_gated(3, True)
    finish_dg(True)
    own_qg = keep_back(qgc, qg_out, 0)
    own_qg.start()
    for part in range(PARTS):
        gather_near(part, False)
        gather_far(part, False)
        if part > 0:
            grad_gated(part - 1, False)
        if part == 3:
            reduce_near(1)
            reduce_far(0)
        complete(part, False)
        if part < 3:
            weight_term(part)
        if part == 2:
            reduce_near(0)
    grad_gated(3, False)
    finish_dg(False)
    weight_term(3)
    def filter_product(re, im, lane, sign):
        ure = [spec_u[a, re, lane] for a in range(4)]
        uim = [spec_u[a, im, lane] for a in range(4)]
        dre = [spec_d[a, re, lane] for a in range(4)]
        dim = [spec_d[a, im, lane] for a in range(4)]
        after = None
        for d in (3, 2, 1, 0):
            real = sum(ure[a] * dre[a + d] + uim[a] * dim[a + d] for a in range(4 - d))
            imag = sum(ure[a] * dim[a + d] - uim[a] * dre[a + d] for a in range(4 - d))
            if after is None:
                prod[d, re, lane] = real.astype(BF16)
                prod[d, im, lane] = imag.astype(BF16)
            else:
                prod[d, re, lane] = (real + sign * after[1]).astype(BF16)
                prod[d, im, lane] = (imag - sign * after[0]).astype(BF16)
            after = (real, imag)

    over_tiles(filter_product)

    def filter_of(xx):
        return jnp.dot(inv[...], prod[xx], preferred_element_type=F32)

    def filter_term(off, carry):
        xx = lax.rem(x + off, 4)
        fsend[xx] = filter_of(xx).astype(BF16)
        for away in (2, 1, 3, 0):
            zz = lax.rem(zh + away, 4)
            remote(
                fsend.at[xx, rows(zz, ROWS), :], frecv.at[x, rows(zz, ROWS), :], ss_f.at[0], rs_f.at[zz], dp_dev(xx, zh)
            ).start()
        return carry

    lax.fori_loop(1, 4, filter_term, 0)
    fown[...] = filter_of(x)

    def correlate(re, im, lane, sign):
        gre = [spec_g[a, re, lane] for a in range(4)]
        gim = [spec_g[a, im, lane] for a in range(4)]
        dre = [spec_d[a, re, lane] for a in range(4)]
        dim = [spec_d[a, im, lane] for a in range(4)]
        for a in range(4):
            prod[a, re, lane] = sum(gre[i - a] * dre[i] + gim[i - a] * dim[i] for i in range(a, 4)).astype(BF16)
            prod[a, im, lane] = sum(gre[i - a] * dim[i] - gim[i - a] * dre[i] for i in range(a, 4)).astype(BF16)

    over_tiles(correlate)

    def grad_prod(i, send):
        duc[rows(i, BLOCK), :] = jnp.dot(inv[...], prod[i], preferred_element_type=F32).astype(BF16)
        if send:
            send_grad_prod(i)

    def send_grad_prod(i):
        for k in range(4):
            send_back(duc, du_out, 1, i * 4 + k)

    away = (1 - zl) * 2
    grad_prod(away, True)
    reduce_near(2)
    grad_prod(away + 1, False)

    def grad_prod_own(j, carry):
        grad_prod(zl * 2 + j, True)
        return carry

    lax.fori_loop(0, 2, grad_prod_own, 0)
    own_du = keep_back(duc, du_out, 1)
    own_du.start()
    reduce_far(1)
    reduce_near(3)
    def filter_sum(zz):
        wait_recv(frecv.at[0, pl.ds(0, 3 * ROWS), :], ss_f.at[0], rs_f.at[zz])
        total = fown[rows(zz, ROWS), :]
        for off in range(1, 4):
            total = total + frecv[lax.rem(x + off, 4), rows(zz, ROWS), :].astype(F32)
        return total

    opposite = lax.rem(zh + 2, 4)
    fsend2[opposite] = filter_sum(opposite).astype(BF16)
    for start, index, dev in ((0, 0, z_up), (64, 1, z_down)):
        half = pl.ds(start, 64)
        remote(fsend2.at[opposite, half, :], frelay.at[half, :], ss_f.at[1], rs_f.at[5 + index], dev).start()
    send_grad_prod((1 - zl) * 2 + 1)
    reduce_far(2)
    for away, start, index, dev in ((1, 0, 0, z_up), (3, 64, 1, z_down)):
        zz = lax.rem(zh + away, 4)
        half = pl.ds(start, 64)
        fown[rows(zz, ROWS), :] = filter_sum(zz)
        wait_recv(frelay.at[half, :], ss_f.at[1], rs_f.at[5 + index])
        fown[pl.ds(pl.multiple_of(zz * ROWS + start, 64), 64), :] += frelay[half, :].astype(F32)
        fsend2[zz] = fown[rows(zz, ROWS), :].astype(BF16)
        remote(fsend2.at[zz], frecv2.at[index], ss_f.at[1], rs_f.at[4], dev).start()
    grad = filter_sum(zh)

    reduce_far(3)
    own_qg.wait()
    own_du.wait()
    wait_recv(qgc.at[pl.ds(0, 15 * ROWS), :], ss_out.at[0], rs_out.at[0])
    wait_recv(qgc.at[pl.ds(0, 15 * ROWS), :], ss_out.at[1], rs_out.at[1])
    wait_recv(wrecv2, ss_w2.at[0], rs_w2.at[0])
    weight = wown[zh] + wrecv2[0].astype(F32) + wrecv2[1].astype(F32)
    wg_out[...] = weight * (1.0 / 16.0)
    wait_recv(frecv2, ss_f.at[1], rs_f.at[4])
    grad = grad + frecv2[0].astype(F32) + frecv2[1].astype(F32)
    fg_out[...] = grad * (1.0 / 16.0)

    for index in range(2):
        wait_send(uc.at[pl.ds(0, 15 * ROWS), :], ss_in.at[index], rs_in.at[index])
        wait_send(qgc.at[pl.ds(0, 15 * ROWS), :], ss_out.at[index], rs_out.at[index])
    wait_send(taps.at[pl.ds(0, 3 * ROWS), :], ss_par.at[0], rs_par.at[0])
    wait_send(wrows.at[0, pl.ds(0, 192), :], ss_par.at[1], rs_par.at[1])
    wait_send(taps.at[pl.ds(0, 3 * BLOCK), :], ss_par.at[2], rs_par.at[2])
    wait_send(wrows.at[pl.ds(0, 3)], ss_par.at[3], rs_par.at[3])

    def drain(part, carry):
        wait_send(cot.at[part, pl.ds(0, 15 * ROWS), :], ss_ag.at[part], rs_z.at[part])
        wait_send(wsend.at[part, pl.ds(0, 3)], ss_w.at[part], rs_w.at[part])
        return carry

    lax.fori_loop(0, PARTS, drain, 0)
    wait_send(wsend2.at[pl.ds(0, 3)], ss_w2.at[0], rs_w2.at[0])
    wait_send(fsend.at[pl.ds(0, 3)], ss_f.at[0], rs_f.at[0])
    wait_send(fsend2.at[pl.ds(0, 3)], ss_f.at[1], rs_f.at[4])


def shards(query_act, key_act, value_act, out_grad, out_weight, filter_taps):
    fwd, inv = transform_tables()
    anywhere = pl.BlockSpec(memory_space=pl.ANY)
    inside = pl.BlockSpec(memory_space=pltpu.VMEM)
    dma = pltpu.SemaphoreType.DMA

    def vmem(shape, dtype):
        return pltpu.VMEM(shape, dtype)

    query_grad, grad_prod, weight_grad, filter_grad = pl.pallas_call(
        kernel,
        out_shape=(
            jax.ShapeDtypeStruct((ROWS, WIDTH), BF16),
            jax.ShapeDtypeStruct((ROWS, WIDTH), BF16),
            jax.ShapeDtypeStruct((CHAN, PIECE), F32),
            jax.ShapeDtypeStruct((ROWS, CHAN), F32),
        ),
        in_specs=[anywhere] * 8,
        out_specs=(anywhere, anywhere, inside, inside),
        scratch_shapes=[
            vmem((2, ROWS, WIDTH), BF16),
            vmem((ROWS, WIDTH), BF16),
            vmem((2 * BLOCK, BLOCK), BF16),
            vmem((BLOCK, 2 * BLOCK), BF16),
            vmem((PARTS, SEQ, SLAB), BF16),
            vmem((PARTS, CHAN, SLAB), BF16),
            vmem((SEQ, CHAN), BF16),
            vmem((SEQ, CHAN), BF16),
            vmem((SEQ, CHAN), BF16),
            vmem((4, 2 * BLOCK, CHAN), F32),
            vmem((4, 2 * BLOCK, CHAN), F32),
            vmem((4, 2 * BLOCK, CHAN), F32),
            vmem((4, 2 * BLOCK, CHAN), BF16),
            vmem((SEQ, CHAN), F32),
            vmem((SEQ, CHAN), F32),
            vmem((CHAN, SEQ), BF16),
            vmem((SEQ, CHAN), BF16),
            vmem((SEQ, CHAN), BF16),
            vmem((SEQ, CHAN), BF16),
            vmem((PARTS, 4, CHAN, PIECE), BF16),
            vmem((PARTS, 4, CHAN, PIECE), BF16),
            vmem((PARTS, CHAN, PIECE), F32),
            vmem((PARTS, CHAN, PIECE), BF16),
            vmem((2, CHAN, PIECE), BF16),
            vmem((PARTS, CHAN, PIECE), BF16),
            vmem((4, BLOCK, CHAN), BF16),
            vmem((4, BLOCK, CHAN), BF16),
            vmem((BLOCK, CHAN), F32),
            vmem((4, ROWS, CHAN), BF16),
            vmem((2, ROWS, CHAN), BF16),
            vmem((ROWS, CHAN), BF16),
            dma((11,)),
            dma((2,)), dma((2,)),
            dma((4,)), dma((8,)),
            dma((PARTS,)),
            *[dma((PARTS,)) for _ in range(9)],
            dma((PARTS,)), dma((PARTS,)),
            dma((1,)), dma((1,)), dma((PARTS,)),
            dma((2,)), dma((7,)),
            dma((2,)), dma((2,)),
        ],
        compiler_params=pltpu.CompilerParams(
            collective_id=0, has_side_effects=True, vmem_limit_bytes=60 * 1024 * 1024
        ),
        cost_estimate=pl.CostEstimate(flops=16_000_000_000, bytes_accessed=16_000_000, transcendentals=0),
        name="hyena_backward",
    )(query_act, key_act, value_act, out_grad, out_weight, filter_taps, fwd, inv)
    spread = grad_prod.astype(F32)
    key_grad = (spread * value_act.astype(F32)).astype(BF16)
    value_grad = (spread * key_act.astype(F32)).astype(BF16)
    return query_grad, key_grad, value_grad, weight_grad, filter_grad


def solution(mesh):
    return jax.shard_map(
        shards,
        mesh=mesh,
        in_specs=(
            P(("dp", "context"), None),
            P(("dp", "context"), None),
            P(("dp", "context"), None),
            P(("dp", "context"), None),
            P("context", "dp"),
            P("dp", "context"),
        ),
        out_specs=(
            P(("dp", "context"), None),
            P(("dp", "context"), None),
            P(("dp", "context"), None),
            P("context", "dp"),
            P("dp", "context"),
        ),
        check_vma=False,
    )
```

```python
import math

import jax
import jax.numpy as jnp
import numpy as np
from jax import lax
from jax.experimental import pallas as pl
from jax.experimental.pallas import tpu as pltpu
from jax.sharding import PartitionSpec as P

SEQ = 2048
CHAN = 256
ROWS = 128
WIDTH = 4096
BLOCK = 512
PARTS = 4
SLAB = 1024
PIECE = 256
FAR_BY_PAIR = (0, 1, 2)
F32 = jnp.float32
BF16 = jnp.bfloat16
MESH = pl.DeviceIdType.MESH


def transform_tables():
    freq = np.concatenate([np.arange(0, BLOCK, 2), np.arange(1, BLOCK, 2)])
    time = np.arange(BLOCK)
    angle = ((2 * freq[:, None] + 1) * time[None, :] % (4 * BLOCK)) * (math.pi / (2 * BLOCK))
    table = np.concatenate([np.cos(angle), -np.sin(angle)], axis=0)
    return jnp.asarray(table, BF16), jnp.asarray(table.T / BLOCK, BF16)


def kernel(
    q_in, k_in, v_in, og_in, w_in, h_in, fwd_in, inv_in,
    qg_out, kg_out, vg_out, wg_out, fg_out,
    kv, ub, fwd, inv, cot, wrows, taps, qc, uc, spec_u, spec_g, spec_d, prod, zbuf, dgbuf, gtr, dzb, qgc, duc, dul,
    wsend, wrecv, wown, wsend2, wrecv2, fsend, frecv, fown, fsend2, frecv2,
    lsem, ss_in, rs_in, ss_par, rs_par, ss_ag, rs_z, rs_ym, rs_yp, rs_zym, rs_zyp, rs_far, rs_sib, rs_zfar, rs_zsib,
    ss_w, rs_w, ss_w2, rs_w2, ss_f, rs_f, ss_out, rs_out,
):
    dp = lax.axis_index("dp")
    ctx = lax.axis_index("context")
    x, zh = dp // 4, dp % 4
    zl, y, core = ctx // 8, (ctx // 2) % 4, ctx % 2

    def ctx_dev(c):
        return {"dp": dp, "context": c}

    def dp_dev(xx, zz):
        return {"dp": xx * 4 + zz, "context": ctx}

    def ctx_of(zz, yy, kk):
        return zz * 8 + lax.rem(yy + 4, 4) * 2 + kk

    def remote(src, dst, send, recv, dev):
        return pltpu.make_async_remote_copy(
            src_ref=src, dst_ref=dst, send_sem=send, recv_sem=recv, device_id=dev, device_id_type=MESH
        )

    me = ctx_dev(lax.rem(ctx + 1, 16))

    def wait_recv(ref, send, recv):
        remote(ref, ref, send, recv, me).wait_recv()

    def wait_send(ref, send, recv):
        remote(ref, ref, send, recv, me).wait_send()

    def cols(i):
        return pl.ds(pl.multiple_of(i * PIECE, PIECE), PIECE)

    def rows(i, n):
        return pl.ds(pl.multiple_of(i * n, n), n)

    local_k = pltpu.make_async_copy(k_in, kv.at[0], lsem.at[0])
    local_v = pltpu.make_async_copy(v_in, kv.at[1], lsem.at[1])
    local_k.start()
    local_v.start()
    local_w = pltpu.make_async_copy(w_in, wrows.at[zh, :, cols(x)], lsem.at[5])
    local_h = pltpu.make_async_copy(h_in, taps.at[rows(dp, ROWS), :], lsem.at[6])
    local_h.start()
    local_w.start()
    local_q = pltpu.make_async_copy(q_in.at[:, cols(ctx)], qc.at[rows(ctx, ROWS), :], lsem.at[7])
    local_q.start()
    for part in range(PARTS):
        for xx in range(4):
            pltpu.make_async_copy(
                og_in.at[:, pl.ds((xx * 4 + part) * PIECE, PIECE)],
                cot.at[part, rows(ctx, ROWS), pl.ds(xx * PIECE, PIECE)],
                lsem.at[4],
            ).start()
    local_fwd = pltpu.make_async_copy(fwd_in, fwd, lsem.at[2])
    local_inv = pltpu.make_async_copy(inv_in, inv, lsem.at[3])
    local_fwd.start()
    local_inv.start()

    barrier = pltpu.get_barrier_semaphore()

    def greet(off, carry):
        pl.semaphore_signal(barrier, inc=1, device_id=ctx_dev(lax.rem(ctx + off, 16)), device_id_type=MESH)
        return carry

    lax.fori_loop(1, 16, greet, 0)
    for off in range(1, 4):
        pl.semaphore_signal(barrier, inc=1, device_id=dp_dev(lax.rem(x + off, 4), zh), device_id_type=MESH)
        pl.semaphore_signal(barrier, inc=1, device_id=dp_dev(x, lax.rem(zh + off, 4)), device_id_type=MESH)
    pl.semaphore_wait(barrier, 21)

    local_h.wait()
    z_up = dp_dev(x, lax.rem(zh + 1, 4))
    z_down = dp_dev(x, lax.rem(zh + 3, 4))

    def send_taps(zz, start, count, index, dev):
        piece = taps.at[pl.ds(pl.multiple_of((x * 4 + zz) * ROWS + start, 64), count), :]
        remote(piece, piece, ss_par.at[0], rs_par.at[index], dev).start()

    def send_rows(zz, start, count, index, dev):
        piece = wrows.at[zz, pl.ds(start, count), cols(x)]
        remote(piece, piece, ss_par.at[1], rs_par.at[index], dev).start()

    send_taps(zh, 0, ROWS, 0, z_up)
    send_taps(zh, 0, ROWS, 1, z_down)

    local_w.wait()
    send_rows(zh, 0, CHAN, 3, z_up)
    send_rows(zh, 0, CHAN, 4, z_down)

    local_k.wait()
    local_v.wait()

    def product(i, carry):
        piece = cols(i)
        ub[:, piece] = (kv[0, :, piece].astype(F32) * kv[1, :, piece].astype(F32)).astype(BF16)
        return carry

    lax.fori_loop(0, 16, product, 0)
    local_u = pltpu.make_async_copy(ub.at[:, cols(ctx)], uc.at[rows(ctx, ROWS), :], lsem.at[8])
    local_u.start()

    dev_z = ctx_dev(ctx_of(1 - zl, y, core))
    dev_up = ctx_dev(ctx_of(zl, y + 1, core))
    dev_down = ctx_dev(ctx_of(zl, y - 1, core))
    dev_sib = ctx_dev(ctx_of(zl, y, 1 - core))

    def spread(part, c, start, count, recv, dev):
        piece = cot.at[part, pl.ds(pl.multiple_of(c * ROWS + start, 64), count), :]
        remote(piece, piece, ss_ag.at[part], recv.at[part], dev).start()

    def arrived(part, count, recv):
        wait_recv(cot.at[part, pl.ds(0, count), :], ss_ag.at[part], recv.at[part])

    def gather_own_z(part):
        spread(part, ctx, 0, ROWS, rs_z, dev_z)

    def gather_own_y(part):
        spread(part, ctx, 0, ROWS, rs_ym, dev_up)
        spread(part, ctx, 0, ROWS, rs_yp, dev_down)
        spread(part, ctx, 0, ROWS, rs_sib, dev_sib)

    def gather_pair(part):
        arrived(part, ROWS, rs_z)
        c = ctx_of(1 - zl, y, core)
        spread(part, c, 0, ROWS, rs_zym, dev_up)
        spread(part, c, 0, ROWS, rs_zyp, dev_down)
        spread(part, c, 0, ROWS, rs_zsib, dev_sib)

    def gather_near(part, own):
        zz = zl if own else 1 - zl
        from_down, from_up = (rs_ym, rs_yp) if own else (rs_zym, rs_zyp)
        far, sib = (rs_far, rs_sib) if own else (rs_zfar, rs_zsib)
        halves = own or part not in FAR_BY_PAIR
        arrived(part, ROWS, from_down)
        c = ctx_of(zz, y - 1, core)
        if halves:
            spread(part, c, 0, 64, far, dev_up)
        spread(part, c, 0, ROWS, sib, dev_sib)
        arrived(part, ROWS, from_up)
        c = ctx_of(zz, y + 1, core)
        if halves:
            spread(part, c, 64, 64, far, dev_down)
        spread(part, c, 0, ROWS, sib, dev_sib)

    def gather_far(part, own):
        zz = zl if own else 1 - zl
        far, sib = (rs_far, rs_sib) if own else (rs_zfar, rs_zsib)
        arrived(part, ROWS, far)
        c = ctx_of(zz, y + 2, core)
        if own and part in FAR_BY_PAIR:
            spread(part, c, 0, ROWS, rs_zfar, dev_z)
        spread(part, c, 0, ROWS, sib, dev_sib)

    def complete(part, own):
        arrived(part, 4 * ROWS, rs_sib if own else rs_zsib)

    pltpu.make_async_copy(cot.at[0, pl.ds(0, 512), :], cot.at[0, pl.ds(0, 512), :], lsem.at[4]).wait()
    gather_own_y(0)
    gather_own_y(1)
    gather_own_y(2)
    for start, recv, dev, away in ((0, 0, z_up, 3), (64, 1, z_down, 1)):
        wait_recv(taps.at[pl.ds(0, ROWS), :], ss_par.at[0], rs_par.at[recv])
        send_taps(lax.rem(zh + away, 4), start, 64, 2, dev)
    for start, recv, dev, away in ((0, 3, z_up, 3), (128, 4, z_down, 1)):
        wait_recv(wrows.at[0, pl.ds(0, 64), :], ss_par.at[1], rs_par.at[recv])
        send_rows(lax.rem(zh + away, 4), start, 128, 5, dev)

    def send_input(source, target, index):
        def step(off, carry):
            for zz in (1 - zl, zl):
                c = zz * 8 + lax.rem(ctx + off, 8)

                @pl.when(c != ctx)
                def _():
                    remote(
                        source.at[:, cols(c)], target.at[rows(ctx, ROWS), :], ss_in.at[index], rs_in.at[index], ctx_dev(c)
                    ).start()

            return carry

        lax.fori_loop(0, 8, step, 0)

    gather_own_z(0)
    send_input(ub, uc, 1)
    gather_own_z(1)
    gather_near(0, True)

    wait_recv(taps.at[pl.ds(0, ROWS), :], ss_par.at[0], rs_par.at[2])
    for off in range(1, 4):
        own = taps.at[rows(x, BLOCK), :]
        remote(own, own, ss_par.at[2], rs_par.at[6], dp_dev(lax.rem(x + off, 4), zh)).start()
    wait_recv(wrows.at[0, pl.ds(0, 64), :], ss_par.at[1], rs_par.at[5])
    for off in range(1, 4):
        own = wrows.at[:, :, cols(x)]
        remote(own, own, ss_par.at[3], rs_par.at[7], dp_dev(lax.rem(x + off, 4), zh)).start()
    gather_near(1, True)
    gather_pair(0)
    send_input(q_in, qc, 0)
    gather_near(2, True)

    def forward(source, spec, first, count):
        def step(j, carry):
            i = first + j
            spec[i] = jnp.dot(fwd[...], source[rows(i, BLOCK), :], preferred_element_type=F32)
            return carry

        lax.fori_loop(0, count, step, 0)

    def over_tiles(body):
        for half in range(2):
            sign = 1.0 - 2.0 * half

            def step(i, carry):
                base = pl.multiple_of(half * 256 + i * 16, 16)
                for lane in range(2):
                    body(pl.ds(base, 16), pl.ds(base + BLOCK, 16), pl.ds(lane * 128, 128), sign)
                return carry

            lax.fori_loop(0, 16, step, 0)

    local_fwd.wait()
    local_inv.wait()
    wait_recv(taps.at[pl.ds(0, 3 * BLOCK), :], ss_par.at[2], rs_par.at[6])
    forward(taps, spec_g, 0, 4)

    def window(re, im, lane, sign):
        for d in (3, 2, 1):
            real = spec_g[d, re, lane] - sign * spec_g[d - 1, im, lane]
            imag = spec_g[d, im, lane] + sign * spec_g[d - 1, re, lane]
            spec_g[d, re, lane] = real
            spec_g[d, im, lane] = imag

    over_tiles(window)

    local_u.wait()
    wait_recv(uc.at[pl.ds(0, 15 * ROWS), :], ss_in.at[1], rs_in.at[1])
    forward(uc, spec_u, 0, 4)

    def convolve(re, im, lane, sign):
        ure = [spec_u[a, re, lane] for a in range(4)]
        uim = [spec_u[a, im, lane] for a in range(4)]
        gre = [spec_g[a, re, lane] for a in range(4)]
        gim = [spec_g[a, im, lane] for a in range(4)]
        for i in range(4):
            prod[i, re, lane] = sum(ure[a] * gre[i - a] - uim[a] * gim[i - a] for a in range(i + 1)).astype(BF16)
            prod[i, im, lane] = sum(ure[a] * gim[i - a] + uim[a] * gre[i - a] for a in range(i + 1)).astype(BF16)

    over_tiles(convolve)
    def conv_out(i, carry):
        out = jnp.dot(inv[...], prod[i], preferred_element_type=F32)
        zbuf[rows(i, BLOCK), :] = out
        return carry

    gather_pair(1)
    gather_own_z(2)
    gather_own_z(3)
    lax.fori_loop(0, 4, conv_out, 0)
    local_q.wait()
    wait_recv(qc.at[pl.ds(0, 15 * ROWS), :], ss_in.at[0], rs_in.at[0])

    def gate(i, carry):
        block = rows(i, 256)
        gated = (qc[block, :].astype(F32) * zbuf[block, :]).astype(BF16).astype(F32)
        gtr[:, block] = gated.T.astype(BF16)
        dgbuf[block, :] = jnp.zeros((256, CHAN), F32)
        return carry

    lax.fori_loop(0, 8, gate, 0)

    def reduce_slab(part):
        wait_recv(wrecv.at[part, pl.ds(0, 3)], ss_w.at[part], rs_w.at[part])
        total = wown[part]
        for off in range(1, 4):
            total = total + wrecv[part, lax.rem(x + off, 4)].astype(F32)
        wown[part] = total

        @pl.when(zh != part)
        def _():
            wsend2[part] = total.astype(BF16)
            remote(wsend2.at[part], wrecv2.at[zh], ss_w2.at[0], rs_w2.at[0], dp_dev(x, part)).start()

    def weight_term(part):
        def product_of(xx):
            return jnp.dot(gtr[...], cot[part, :, cols(xx)], preferred_element_type=F32)

        def step(off, carry):
            xx = lax.rem(x + off, 4)
            wsend[part, xx] = product_of(xx).astype(BF16)
            remote(wsend.at[part, xx], wrecv.at[part, x], ss_w.at[part], rs_w.at[part], dp_dev(xx, zh)).start()
            return carry

        lax.fori_loop(1, 4, step, 0)
        wown[part] = product_of(x)

    def grad_gated(part, own):
        zz = zl if own else 1 - zl

        def step(i, carry):
            block = rows(zz * 2 + i, BLOCK)
            dgbuf[block, :] += lax.dot_general(
                cot[part, block, :], wrows[part], (((1,), (1,)), ((), ())), preferred_element_type=F32
            )
            return carry

        lax.fori_loop(0, 2, step, 0)

    def send_back(source, target, index, c):
        @pl.when(c != ctx)
        def _():
            remote(
                source.at[rows(c, ROWS), :], target.at[:, cols(ctx)], ss_out.at[index], rs_out.at[index], ctx_dev(c)
            ).start()

    def keep_back(source, target, index):
        return pltpu.make_async_copy(source.at[rows(ctx, ROWS), :], target.at[:, cols(ctx)], lsem.at[9 + index])

    def finish_dg(own):
        zz = zl if own else 1 - zl

        def step(off, carry):
            c = zz * 8 + lax.rem(ctx + off, 8)
            block = rows(c, ROWS)
            grad = dgbuf[block, :]
            qgc[block, :] = (grad * zbuf[block, :]).astype(BF16)
            dzb[block, :] = (grad * qc[block, :].astype(F32)).astype(BF16)
            send_back(qgc, qg_out, 0, c)
            return carry

        lax.fori_loop(0, 8, step, 0)
        forward(dzb, spec_d, zz * 2, 2)

    gather_far(0, True)
    gather_far(1, True)
    gather_pair(2)
    gather_far(2, True)
    wait_recv(wrows.at[pl.ds(0, 3)], ss_par.at[3], rs_par.at[7])
    complete(0, True)
    grad_gated(0, True)
    gather_pair(3)
    complete(1, True)
    grad_gated(1, True)
    complete(2, True)
    grad_gated(2, True)
    gather_near(0, False)
    gather_far(0, False)
    gather_near(1, False)
    gather_near(2, False)
    complete(0, False)
    weight_term(0)
    grad_gated(0, False)
    gather_near(3, False)
    gather_own_y(3)
    gather_far(1, False)
    complete(1, False)
    weight_term(1)
    grad_gated(1, False)
    gather_far(2, False)
    gather_far(3, False)
    complete(2, False)
    grad_gated(2, False)
    complete(3, False)
    grad_gated(3, False)
    gather_near(3, True)
    finish_dg(False)
    reduce_slab(0)
    weight_term(2)
    gather_far(3, True)
    reduce_slab(1)
    complete(3, True)
    grad_gated(3, True)
    finish_dg(True)
    own_qg = keep_back(qgc, qg_out, 0)
    own_qg.start()
    reduce_slab(2)
    def correlate(re, im, lane, sign):
        gre = [spec_g[a, re, lane] for a in range(4)]
        gim = [spec_g[a, im, lane] for a in range(4)]
        dre = [spec_d[a, re, lane] for a in range(4)]
        dim = [spec_d[a, im, lane] for a in range(4)]
        for a in range(4):
            prod[a, re, lane] = sum(gre[i - a] * dre[i] + gim[i - a] * dim[i] for i in range(a, 4)).astype(BF16)
            prod[a, im, lane] = sum(gre[i - a] * dim[i] - gim[i - a] * dre[i] for i in range(a, 4)).astype(BF16)

    over_tiles(correlate)

    def grad_prod(i, carry):
        duc[rows(i, BLOCK), :] = jnp.dot(inv[...], prod[i], preferred_element_type=F32).astype(BF16)
        return carry

    lax.fori_loop(0, 4, grad_prod, 0)

    def send_grad_prod(off, carry):
        c = lax.rem(ctx + off, 8)
        send_back(duc, dul, 1, (1 - zl) * 8 + c)
        send_back(duc, dul, 1, zl * 8 + c)
        return carry

    lax.fori_loop(0, 8, send_grad_prod, 0)
    own_du = keep_back(duc, dul, 1)
    own_du.start()
    weight_term(3)

    def filter_product(re, im, lane, sign):
        ure = [spec_u[a, re, lane] for a in range(4)]
        uim = [spec_u[a, im, lane] for a in range(4)]
        dre = [spec_d[a, re, lane] for a in range(4)]
        dim = [spec_d[a, im, lane] for a in range(4)]
        after = None
        for d in (3, 2, 1, 0):
            real = sum(ure[a] * dre[a + d] + uim[a] * dim[a + d] for a in range(4 - d))
            imag = sum(ure[a] * dim[a + d] - uim[a] * dre[a + d] for a in range(4 - d))
            if after is None:
                prod[d, re, lane] = real.astype(BF16)
                prod[d, im, lane] = imag.astype(BF16)
            else:
                prod[d, re, lane] = (real + sign * after[1]).astype(BF16)
                prod[d, im, lane] = (imag - sign * after[0]).astype(BF16)
            after = (real, imag)

    over_tiles(filter_product)

    def filter_of(xx):
        return jnp.dot(inv[...], prod[xx], preferred_element_type=F32)

    def filter_term(off, carry):
        xx = lax.rem(x + off, 4)
        fsend[xx] = filter_of(xx).astype(BF16)
        for away in (2, 1, 3, 0):
            zz = lax.rem(zh + away, 4)
            remote(
                fsend.at[xx, rows(zz, ROWS), :], frecv.at[x, rows(zz, ROWS), :], ss_f.at[0], rs_f.at[zz], dp_dev(xx, zh)
            ).start()
        return carry

    lax.fori_loop(1, 4, filter_term, 0)
    fown[...] = filter_of(x)

    reduce_slab(3)
    def filter_sum(zz):
        wait_recv(frecv.at[0, pl.ds(0, 3 * ROWS), :], ss_f.at[0], rs_f.at[zz])
        total = fown[rows(zz, ROWS), :]
        for off in range(1, 4):
            total = total + frecv[lax.rem(x + off, 4), rows(zz, ROWS), :].astype(F32)
        return total

    for away in (2, 1, 3):
        zz = lax.rem(zh + away, 4)
        fsend2[zz] = filter_sum(zz).astype(BF16)
        remote(fsend2.at[zz], frecv2.at[zh], ss_f.at[1], rs_f.at[4], dp_dev(x, zz)).start()
    grad = filter_sum(zh)

    own_qg.wait()
    own_du.wait()
    wait_recv(qgc.at[pl.ds(0, 15 * ROWS), :], ss_out.at[0], rs_out.at[0])
    wait_recv(qgc.at[pl.ds(0, 15 * ROWS), :], ss_out.at[1], rs_out.at[1])
    def branch_grads(i, carry):
        piece = cols(i)
        grad = dul[:, piece].astype(F32)
        value = (grad * kv[0, :, piece].astype(F32)).astype(BF16)
        kv[0, :, piece] = (grad * kv[1, :, piece].astype(F32)).astype(BF16)
        kv[1, :, piece] = value
        return carry

    lax.fori_loop(0, 16, branch_grads, 0)
    write_k = pltpu.make_async_copy(kv.at[0], kg_out, lsem.at[0])
    write_v = pltpu.make_async_copy(kv.at[1], vg_out, lsem.at[1])
    write_k.start()
    write_v.start()
    wait_recv(wrecv2.at[pl.ds(0, 3)], ss_w2.at[0], rs_w2.at[0])
    weight = wown[zh]
    for off in range(1, 4):
        weight = weight + wrecv2[lax.rem(zh + off, 4)].astype(F32)
    wg_out[...] = weight * (1.0 / 16.0)
    wait_recv(frecv2.at[pl.ds(0, 3)], ss_f.at[1], rs_f.at[4])
    for off in range(1, 4):
        grad = grad + frecv2[lax.rem(zh + off, 4)].astype(F32)
    fg_out[...] = grad * (1.0 / 16.0)

    write_k.wait()
    write_v.wait()
    for index in range(2):
        wait_send(uc.at[pl.ds(0, 15 * ROWS), :], ss_in.at[index], rs_in.at[index])
        wait_send(qgc.at[pl.ds(0, 15 * ROWS), :], ss_out.at[index], rs_out.at[index])
    wait_send(taps.at[pl.ds(0, 3 * ROWS), :], ss_par.at[0], rs_par.at[0])
    wait_send(wrows.at[0, pl.ds(0, 192), :], ss_par.at[1], rs_par.at[1])
    wait_send(taps.at[pl.ds(0, 3 * BLOCK), :], ss_par.at[2], rs_par.at[2])
    wait_send(wrows.at[pl.ds(0, 3)], ss_par.at[3], rs_par.at[3])

    def drain(part, carry):
        wait_send(cot.at[part, pl.ds(0, 15 * ROWS), :], ss_ag.at[part], rs_z.at[part])
        wait_send(wsend.at[part, pl.ds(0, 3)], ss_w.at[part], rs_w.at[part])
        return carry

    lax.fori_loop(0, PARTS, drain, 0)
    wait_send(wsend2.at[pl.ds(0, 3)], ss_w2.at[0], rs_w2.at[0])
    wait_send(fsend.at[pl.ds(0, 3)], ss_f.at[0], rs_f.at[0])
    wait_send(fsend2.at[pl.ds(0, 3)], ss_f.at[1], rs_f.at[4])


def hand_over(*refs):
    sources, targets, stage, (load_sem, store_sem) = refs[:5], refs[5:10], refs[10:15], refs[15:]
    loads, stores = [], []
    for i, source in enumerate(sources):
        parts = 2 if source.shape[1] == WIDTH else 1
        count = source.shape[0] // parts
        for part in range(parts):
            piece = pl.ds(part * count, count)
            n = len(loads)
            loads.append(pltpu.make_async_copy(source.at[piece], stage[i].at[piece], load_sem.at[n]))
            stores.append(pltpu.make_async_copy(stage[i].at[piece], targets[i].at[piece], store_sem.at[n]))
    for load in loads:
        load.start()
    for load, store in zip(loads, stores):
        load.wait()
        store.start()
    for store in stores:
        store.wait()


def shards(query_act, key_act, value_act, out_grad, out_weight, filter_taps):
    fwd, inv = transform_tables()
    anywhere = pl.BlockSpec(memory_space=pl.ANY)
    inside = pl.BlockSpec(memory_space=pltpu.VMEM)
    dma = pltpu.SemaphoreType.DMA

    def vmem(shape, dtype):
        return pltpu.VMEM(shape, dtype)

    outs = (
        jax.ShapeDtypeStruct((ROWS, WIDTH), BF16),
        jax.ShapeDtypeStruct((ROWS, WIDTH), BF16),
        jax.ShapeDtypeStruct((ROWS, WIDTH), BF16),
        jax.ShapeDtypeStruct((CHAN, PIECE), F32),
        jax.ShapeDtypeStruct((ROWS, CHAN), F32),
    )
    grads = pl.pallas_call(
        kernel,
        out_shape=outs,
        in_specs=[anywhere] * 8,
        out_specs=(anywhere, anywhere, anywhere, inside, inside),
        scratch_shapes=[
            vmem((2, ROWS, WIDTH), BF16),
            vmem((ROWS, WIDTH), BF16),
            vmem((2 * BLOCK, BLOCK), BF16),
            vmem((BLOCK, 2 * BLOCK), BF16),
            vmem((PARTS, SEQ, SLAB), BF16),
            vmem((PARTS, CHAN, SLAB), BF16),
            vmem((SEQ, CHAN), BF16),
            vmem((SEQ, CHAN), BF16),
            vmem((SEQ, CHAN), BF16),
            vmem((4, 2 * BLOCK, CHAN), F32),
            vmem((4, 2 * BLOCK, CHAN), F32),
            vmem((4, 2 * BLOCK, CHAN), F32),
            vmem((4, 2 * BLOCK, CHAN), BF16),
            vmem((SEQ, CHAN), F32),
            vmem((SEQ, CHAN), F32),
            vmem((CHAN, SEQ), BF16),
            vmem((SEQ, CHAN), BF16),
            vmem((SEQ, CHAN), BF16),
            vmem((SEQ, CHAN), BF16),
            vmem((ROWS, WIDTH), BF16),
            vmem((PARTS, 4, CHAN, PIECE), BF16),
            vmem((PARTS, 4, CHAN, PIECE), BF16),
            vmem((PARTS, CHAN, PIECE), F32),
            vmem((PARTS, CHAN, PIECE), BF16),
            vmem((4, CHAN, PIECE), BF16),
            vmem((4, BLOCK, CHAN), BF16),
            vmem((4, BLOCK, CHAN), BF16),
            vmem((BLOCK, CHAN), F32),
            vmem((4, ROWS, CHAN), BF16),
            vmem((4, ROWS, CHAN), BF16),
            dma((11,)),
            dma((2,)), dma((2,)),
            dma((4,)), dma((8,)),
            dma((PARTS,)),
            *[dma((PARTS,)) for _ in range(9)],
            dma((PARTS,)), dma((PARTS,)),
            dma((1,)), dma((1,)),
            dma((2,)), dma((5,)),
            dma((2,)), dma((2,)),
        ],
        compiler_params=pltpu.CompilerParams(
            collective_id=0, has_side_effects=True, vmem_limit_bytes=60 * 1024 * 1024
        ),
        cost_estimate=pl.CostEstimate(flops=16_000_000_000, bytes_accessed=16_000_000, transcendentals=0),
        name="hyena_backward",
    )(query_act, key_act, value_act, out_grad, out_weight, filter_taps, fwd, inv)
    return pl.pallas_call(
        hand_over,
        out_shape=outs,
        in_specs=[anywhere] * 5,
        out_specs=(anywhere,) * 5,
        scratch_shapes=[vmem(out.shape, out.dtype) for out in outs] + [dma((8,)), dma((8,))],
        compiler_params=pltpu.CompilerParams(vmem_limit_bytes=60 * 1024 * 1024),
        cost_estimate=pl.CostEstimate(flops=0, bytes_accessed=7_000_000, transcendentals=0),
        name="hand_over",
    )(*grads)


def solution(mesh):
    return jax.shard_map(
        shards,
        mesh=mesh,
        in_specs=(
            P(("dp", "context"), None),
            P(("dp", "context"), None),
            P(("dp", "context"), None),
            P(("dp", "context"), None),
            P("context", "dp"),
            P("dp", "context"),
        ),
        out_specs=(
            P(("dp", "context"), None),
            P(("dp", "context"), None),
            P(("dp", "context"), None),
            P("context", "dp"),
            P("dp", "context"),
        ),
        check_vma=False,
    )
```

```python
import math

import jax
import jax.numpy as jnp
import numpy as np
from jax import lax
from jax.experimental import pallas as pl
from jax.experimental.pallas import tpu as pltpu
from jax.sharding import PartitionSpec as P

SEQ = 2048
CHAN = 256
ROWS = 128
WIDTH = 4096
BLOCK = 512
PARTS = 4
SLAB = 1024
PIECE = 256
HALF = 128
FAR_BY_PAIR = (0, 1, 2)
F32 = jnp.float32
BF16 = jnp.bfloat16
MESH = pl.DeviceIdType.MESH


def transform_tables():
    freq = np.concatenate([np.arange(0, BLOCK, 2), np.arange(1, BLOCK, 2)])
    time = np.arange(BLOCK)
    angle = ((2 * freq[:, None] + 1) * time[None, :] % (4 * BLOCK)) * (math.pi / (2 * BLOCK))
    table = np.concatenate([np.cos(angle), -np.sin(angle)], axis=0)
    return jnp.asarray(table, BF16), jnp.asarray(table.T / BLOCK, BF16)


def kernel(
    q_in, k_in, v_in, og_in, w_in, h_in, fwd_in, inv_in,
    qg_out, kg_out, vg_out, wg_out, fg_out,
    kv, ub, fwd, inv, cot, wrows, taps, qc, uc, spec_u, spec_g, spec_d, prod, zbuf, dgbuf, gtr, qgc, duc, dul,
    wsend, wrecv, wown, wsend2, wrecv2, wfin, fsend, frecv, fown, fsend2, frecv2,
    lsem, ss_in, rs_in, ss_par, rs_par, ss_ag, rs_z, rs_ym, rs_yp, rs_zym, rs_zyp, rs_far, rs_sib, rs_zfar, rs_zsib,
    ss_w, rs_w, ss_w2, rs_w2, ss_f, rs_f, ss_out, rs_out,
):
    dp = lax.axis_index("dp")
    ctx = lax.axis_index("context")
    x, zh = dp // 4, dp % 4
    zl, y, core = ctx // 8, (ctx // 2) % 4, ctx % 2

    def ctx_dev(c):
        return {"dp": dp, "context": c}

    def dp_dev(xx, zz):
        return {"dp": xx * 4 + zz, "context": ctx}

    def ctx_of(zz, yy, kk):
        return zz * 8 + lax.rem(yy + 4, 4) * 2 + kk

    def remote(src, dst, send, recv, dev):
        return pltpu.make_async_remote_copy(
            src_ref=src, dst_ref=dst, send_sem=send, recv_sem=recv, device_id=dev, device_id_type=MESH
        )

    me = ctx_dev(lax.rem(ctx + 1, 16))

    def wait_recv(ref, send, recv):
        remote(ref, ref, send, recv, me).wait_recv()

    def wait_send(ref, send, recv):
        remote(ref, ref, send, recv, me).wait_send()

    def cols(i):
        return pl.ds(pl.multiple_of(i * PIECE, PIECE), PIECE)

    def rows(i, n):
        return pl.ds(pl.multiple_of(i * n, n), n)

    local_k = pltpu.make_async_copy(k_in, kv.at[0], lsem.at[0])
    local_v = pltpu.make_async_copy(v_in, kv.at[1], lsem.at[1])
    local_k.start()
    local_v.start()
    def side_of(zz):
        return pl.ds(pl.multiple_of(x * PIECE + zz // 2 * HALF, HALF), HALF)

    local_w = [
        pltpu.make_async_copy(
            w_in.at[:, pl.ds(half * HALF, HALF)], wrows.at[lax.rem(zh, 2) * 2 + half, :, side_of(zh)], lsem.at[5]
        )
        for half in range(2)
    ]
    local_h = pltpu.make_async_copy(h_in, taps.at[rows(dp, ROWS), :], lsem.at[6])
    local_h.start()
    for copy in local_w:
        copy.start()
    local_q = pltpu.make_async_copy(q_in.at[:, cols(ctx)], qc.at[rows(ctx, ROWS), :], lsem.at[7])
    local_q.start()
    for part in range(PARTS):
        for xx in range(4):
            for side in range(2):
                pltpu.make_async_copy(
                    og_in.at[:, pl.ds((xx * 4 + part // 2 + 2 * side) * PIECE + part % 2 * HALF, HALF)],
                    cot.at[part, rows(ctx, ROWS), pl.ds(xx * PIECE + side * HALF, HALF)],
                    lsem.at[4],
                ).start()
    local_fwd = pltpu.make_async_copy(fwd_in, fwd, lsem.at[2])
    local_inv = pltpu.make_async_copy(inv_in, inv, lsem.at[3])
    local_fwd.start()
    local_inv.start()

    barrier = pltpu.get_barrier_semaphore()

    def greet(off, carry):
        pl.semaphore_signal(barrier, inc=1, device_id=ctx_dev(lax.rem(ctx + off, 16)), device_id_type=MESH)
        return carry

    lax.fori_loop(1, 16, greet, 0)
    for off in range(1, 4):
        pl.semaphore_signal(barrier, inc=1, device_id=dp_dev(lax.rem(x + off, 4), zh), device_id_type=MESH)
        pl.semaphore_signal(barrier, inc=1, device_id=dp_dev(x, lax.rem(zh + off, 4)), device_id_type=MESH)
    pl.semaphore_wait(barrier, 21)

    local_h.wait()
    z_up = dp_dev(x, lax.rem(zh + 1, 4))
    z_down = dp_dev(x, lax.rem(zh + 3, 4))

    def send_taps(zz, start, count, index, dev):
        piece = taps.at[pl.ds(pl.multiple_of((x * 4 + zz) * ROWS + start, 64), count), :]
        remote(piece, piece, ss_par.at[0], rs_par.at[index], dev).start()

    def send_rows(zz, start, count, index, dev):
        piece = wrows.at[pl.ds(lax.rem(zz, 2) * 2, 2), pl.ds(start, count), side_of(zz)]
        remote(piece, piece, ss_par.at[1], rs_par.at[index], dev).start()

    send_taps(zh, 0, ROWS, 0, z_up)
    send_taps(zh, 0, ROWS, 1, z_down)

    pltpu.make_async_copy(w_in, w_in, lsem.at[5]).wait()
    send_rows(zh, 0, CHAN, 3, z_up)
    send_rows(zh, 0, CHAN, 4, z_down)

    local_k.wait()
    local_v.wait()

    def product(i, carry):
        piece = cols(i)
        ub[:, piece] = (kv[0, :, piece].astype(F32) * kv[1, :, piece].astype(F32)).astype(BF16)
        return carry

    lax.fori_loop(0, 16, product, 0)
    local_u = pltpu.make_async_copy(ub.at[:, cols(ctx)], uc.at[rows(ctx, ROWS), :], lsem.at[8])
    local_u.start()

    dev_z = ctx_dev(ctx_of(1 - zl, y, core))
    dev_up = ctx_dev(ctx_of(zl, y + 1, core))
    dev_down = ctx_dev(ctx_of(zl, y - 1, core))
    dev_sib = ctx_dev(ctx_of(zl, y, 1 - core))

    def spread(part, c, start, count, recv, dev):
        piece = cot.at[part, pl.ds(pl.multiple_of(c * ROWS + start, 64), count), :]
        remote(piece, piece, ss_ag.at[part], recv.at[part], dev).start()

    def arrived(part, count, recv):
        wait_recv(cot.at[part, pl.ds(0, count), :], ss_ag.at[part], recv.at[part])

    def gather_own_z(part):
        spread(part, ctx, 0, ROWS, rs_z, dev_z)

    def gather_own_y(part):
        spread(part, ctx, 0, ROWS, rs_ym, dev_up)
        spread(part, ctx, 0, ROWS, rs_yp, dev_down)
        spread(part, ctx, 0, ROWS, rs_sib, dev_sib)

    def gather_pair(part):
        arrived(part, ROWS, rs_z)
        c = ctx_of(1 - zl, y, core)
        spread(part, c, 0, ROWS, rs_zym, dev_up)
        spread(part, c, 0, ROWS, rs_zyp, dev_down)
        spread(part, c, 0, ROWS, rs_zsib, dev_sib)

    def gather_near(part, own):
        zz = zl if own else 1 - zl
        from_down, from_up = (rs_ym, rs_yp) if own else (rs_zym, rs_zyp)
        far, sib = (rs_far, rs_sib) if own else (rs_zfar, rs_zsib)
        halves = own or part not in FAR_BY_PAIR
        arrived(part, ROWS, from_down)
        c = ctx_of(zz, y - 1, core)
        if halves:
            spread(part, c, 0, 64, far, dev_up)
        spread(part, c, 0, ROWS, sib, dev_sib)
        arrived(part, ROWS, from_up)
        c = ctx_of(zz, y + 1, core)
        if halves:
            spread(part, c, 64, 64, far, dev_down)
        spread(part, c, 0, ROWS, sib, dev_sib)

    def gather_far(part, own):
        zz = zl if own else 1 - zl
        far, sib = (rs_far, rs_sib) if own else (rs_zfar, rs_zsib)
        arrived(part, ROWS, far)
        c = ctx_of(zz, y + 2, core)
        if own and part in FAR_BY_PAIR:
            spread(part, c, 0, ROWS, rs_zfar, dev_z)
        spread(part, c, 0, ROWS, sib, dev_sib)

    def complete(part, own):
        arrived(part, 4 * ROWS, rs_sib if own else rs_zsib)

    pltpu.make_async_copy(cot.at[0, pl.ds(0, 512), :], cot.at[0, pl.ds(0, 512), :], lsem.at[4]).wait()
    gather_own_y(0)
    gather_own_y(1)
    gather_own_y(2)
    for start, recv, dev, away in ((0, 0, z_up, 3), (64, 1, z_down, 1)):
        wait_recv(taps.at[pl.ds(0, ROWS), :], ss_par.at[0], rs_par.at[recv])
        send_taps(lax.rem(zh + away, 4), start, 64, 2, dev)
    for start, recv, dev, away in ((0, 3, z_up, 3), (128, 4, z_down, 1)):
        wait_recv(wrows.at[0, pl.ds(0, 64), :], ss_par.at[1], rs_par.at[recv])
        send_rows(lax.rem(zh + away, 4), start, 128, 5, dev)

    def send_input(source, target, index):
        def step(off, carry):
            for zz in (1 - zl, zl):
                c = zz * 8 + lax.rem(ctx + off, 8)

                @pl.when(c != ctx)
                def _():
                    remote(
                        source.at[:, cols(c)], target.at[rows(ctx, ROWS), :], ss_in.at[index], rs_in.at[index], ctx_dev(c)
                    ).start()

            return carry

        lax.fori_loop(0, 8, step, 0)

    gather_own_z(0)
    send_input(ub, uc, 1)
    gather_own_z(1)
    gather_near(0, True)

    wait_recv(taps.at[pl.ds(0, ROWS), :], ss_par.at[0], rs_par.at[2])
    for off in range(1, 4):
        own = taps.at[rows(x, BLOCK), :]
        remote(own, own, ss_par.at[2], rs_par.at[6], dp_dev(lax.rem(x + off, 4), zh)).start()
    wait_recv(wrows.at[0, pl.ds(0, 64), :], ss_par.at[1], rs_par.at[5])
    for off in range(1, 4):
        own = wrows.at[:, :, cols(x)]
        remote(own, own, ss_par.at[3], rs_par.at[7], dp_dev(lax.rem(x + off, 4), zh)).start()
    gather_near(1, True)
    gather_pair(0)
    send_input(q_in, qc, 0)
    gather_near(2, True)

    def forward(source, spec, first, count):
        def step(j, carry):
            i = first + j
            spec[i] = jnp.dot(fwd[...], source[rows(i, BLOCK), :], preferred_element_type=F32)
            return carry

        lax.fori_loop(0, count, step, 0)

    def over_tiles(body):
        for half in range(2):
            sign = 1.0 - 2.0 * half

            def step(i, carry):
                base = pl.multiple_of(half * 256 + i * 16, 16)
                for lane in range(2):
                    body(pl.ds(base, 16), pl.ds(base + BLOCK, 16), pl.ds(lane * 128, 128), sign)
                return carry

            lax.fori_loop(0, 16, step, 0)

    local_fwd.wait()
    local_inv.wait()
    wait_recv(taps.at[pl.ds(0, 3 * BLOCK), :], ss_par.at[2], rs_par.at[6])
    forward(taps, spec_g, 0, 4)

    def window(re, im, lane, sign):
        for d in (3, 2, 1):
            real = spec_g[d, re, lane] - sign * spec_g[d - 1, im, lane]
            imag = spec_g[d, im, lane] + sign * spec_g[d - 1, re, lane]
            spec_g[d, re, lane] = real
            spec_g[d, im, lane] = imag

    over_tiles(window)

    local_u.wait()
    wait_recv(uc.at[pl.ds(0, 15 * ROWS), :], ss_in.at[1], rs_in.at[1])
    forward(uc, spec_u, 0, 4)

    def convolve(re, im, lane, sign):
        ure = [spec_u[a, re, lane] for a in range(4)]
        uim = [spec_u[a, im, lane] for a in range(4)]
        gre = [spec_g[a, re, lane] for a in range(4)]
        gim = [spec_g[a, im, lane] for a in range(4)]
        for i in range(4):
            prod[i, re, lane] = sum(ure[a] * gre[i - a] - uim[a] * gim[i - a] for a in range(i + 1)).astype(BF16)
            prod[i, im, lane] = sum(ure[a] * gim[i - a] + uim[a] * gre[i - a] for a in range(i + 1)).astype(BF16)

    over_tiles(convolve)
    def conv_out(i, carry):
        out = jnp.dot(inv[...], prod[i], preferred_element_type=F32)
        zbuf[rows(i, BLOCK), :] = out
        return carry

    gather_pair(1)
    gather_own_z(2)
    gather_own_z(3)
    lax.fori_loop(0, 4, conv_out, 0)
    local_q.wait()
    wait_recv(qc.at[pl.ds(0, 15 * ROWS), :], ss_in.at[0], rs_in.at[0])

    def gate(i, carry):
        block = rows(i, 256)
        gated = (qc[block, :].astype(F32) * zbuf[block, :]).astype(BF16).astype(F32)
        gtr[:, block] = gated.T.astype(BF16)
        dgbuf[block, :] = jnp.zeros((256, CHAN), F32)
        return carry

    lax.fori_loop(0, 8, gate, 0)

    def reduce_slab(part):
        wait_recv(wrecv.at[part, pl.ds(0, 3)], ss_w.at[part], rs_w.at[part])
        total = wown[part]
        for off in range(1, 4):
            total = total + wrecv[part, lax.rem(x + off, 4)].astype(F32)
        wsend2[part] = total.astype(BF16)
        target = pl.ds(part % 2 * HALF, HALF)
        for side in range(2):
            source = pl.ds(side * HALF, HALF)
            zz = part // 2 + 2 * side

            @pl.when(zh == zz)
            def _():
                wfin[:, target] = total[:, side * HALF : (side + 1) * HALF]

            @pl.when(zh != zz)
            def _():
                remote(
                    wsend2.at[part, :, source], wrecv2.at[zh, :, target], ss_w2.at[0], rs_w2.at[0], dp_dev(x, zz)
                ).start()

    def weight_term(part):
        def product_of(xx):
            return jnp.dot(gtr[...], cot[part, :, cols(xx)], preferred_element_type=F32)

        def step(off, carry):
            xx = lax.rem(x + off, 4)
            wsend[part, xx] = product_of(xx).astype(BF16)
            remote(wsend.at[part, xx], wrecv.at[part, x], ss_w.at[part], rs_w.at[part], dp_dev(xx, zh)).start()
            return carry

        lax.fori_loop(1, 4, step, 0)
        wown[part] = product_of(x)

    def grad_gated(part, own):
        zz = zl if own else 1 - zl

        def step(i, carry):
            block = rows(zz * 2 + i, BLOCK)
            dgbuf[block, :] += lax.dot_general(
                cot[part, block, :], wrows[part], (((1,), (1,)), ((), ())), preferred_element_type=F32
            )
            return carry

        lax.fori_loop(0, 2, step, 0)

    def send_back(source, target, index, c):
        @pl.when(c != ctx)
        def _():
            remote(
                source.at[rows(c, ROWS), :], target.at[:, cols(ctx)], ss_out.at[index], rs_out.at[index], ctx_dev(c)
            ).start()

    def keep_back(source, target, index):
        return pltpu.make_async_copy(source.at[rows(ctx, ROWS), :], target.at[:, cols(ctx)], lsem.at[9 + index])

    def finish_dg(own):
        zz = zl if own else 1 - zl

        def step(off, carry):
            c = zz * 8 + lax.rem(ctx + off, 8)
            block = rows(c, ROWS)
            grad = dgbuf[block, :]
            qgc[block, :] = (grad * zbuf[block, :]).astype(BF16)
            qc[block, :] = (grad * qc[block, :].astype(F32)).astype(BF16)
            send_back(qgc, qg_out, 0, c)
            return carry

        lax.fori_loop(0, 8, step, 0)
        forward(qc, spec_d, zz * 2, 2)

    gather_far(0, True)
    gather_far(1, True)
    gather_pair(2)
    gather_far(2, True)
    wait_recv(wrows.at[pl.ds(0, 3)], ss_par.at[3], rs_par.at[7])
    complete(0, True)
    grad_gated(0, True)
    gather_pair(3)
    complete(1, True)
    grad_gated(1, True)
    complete(2, True)
    grad_gated(2, True)
    gather_near(0, False)
    gather_far(0, False)
    gather_near(1, False)
    gather_near(2, False)
    complete(0, False)
    weight_term(0)
    grad_gated(0, False)
    gather_near(3, False)
    gather_own_y(3)
    gather_far(1, False)
    complete(1, False)
    weight_term(1)
    grad_gated(1, False)
    gather_far(2, False)
    gather_far(3, False)
    complete(2, False)
    grad_gated(2, False)
    complete(3, False)
    grad_gated(3, False)
    gather_near(3, True)
    finish_dg(False)
    reduce_slab(0)
    weight_term(2)
    gather_far(3, True)
    reduce_slab(1)
    complete(3, True)
    grad_gated(3, True)
    finish_dg(True)
    own_qg = keep_back(qgc, qg_out, 0)
    own_qg.start()
    reduce_slab(2)
    def filter_product(re, im, lane, sign):
        ure = [spec_u[a, re, lane] for a in range(4)]
        uim = [spec_u[a, im, lane] for a in range(4)]
        dre = [spec_d[a, re, lane] for a in range(4)]
        dim = [spec_d[a, im, lane] for a in range(4)]
        after = None
        for d in (3, 2, 1, 0):
            real = sum(ure[a] * dre[a + d] + uim[a] * dim[a + d] for a in range(4 - d))
            imag = sum(ure[a] * dim[a + d] - uim[a] * dre[a + d] for a in range(4 - d))
            if after is None:
                prod[d, re, lane] = real.astype(BF16)
                prod[d, im, lane] = imag.astype(BF16)
            else:
                prod[d, re, lane] = (real + sign * after[1]).astype(BF16)
                prod[d, im, lane] = (imag - sign * after[0]).astype(BF16)
            after = (real, imag)

    over_tiles(filter_product)

    def filter_of(xx):
        return jnp.dot(inv[...], prod[xx], preferred_element_type=F32)

    def filter_term(off, carry):
        xx = lax.rem(x + off, 4)
        fsend[xx] = filter_of(xx).astype(BF16)
        for away in (2, 1, 3, 0):
            zz = lax.rem(zh + away, 4)
            remote(
                fsend.at[xx, rows(zz, ROWS), :], frecv.at[x, rows(zz, ROWS), :], ss_f.at[0], rs_f.at[zz], dp_dev(xx, zh)
            ).start()
        return carry

    lax.fori_loop(1, 4, filter_term, 0)
    fown[...] = filter_of(x)

    def correlate(re, im, lane, sign):
        gre = [spec_g[a, re, lane] for a in range(4)]
        gim = [spec_g[a, im, lane] for a in range(4)]
        dre = [spec_d[a, re, lane] for a in range(4)]
        dim = [spec_d[a, im, lane] for a in range(4)]
        for a in range(4):
            prod[a, re, lane] = sum(gre[i - a] * dre[i] + gim[i - a] * dim[i] for i in range(a, 4)).astype(BF16)
            prod[a, im, lane] = sum(gre[i - a] * dim[i] - gim[i - a] * dre[i] for i in range(a, 4)).astype(BF16)

    over_tiles(correlate)

    def grad_prod(i, carry):
        duc[rows(i, BLOCK), :] = jnp.dot(inv[...], prod[i], preferred_element_type=F32).astype(BF16)
        return carry

    lax.fori_loop(0, 4, grad_prod, 0)

    def send_grad_prod(off, carry):
        c = lax.rem(ctx + off, 8)
        send_back(duc, dul, 1, (1 - zl) * 8 + c)
        send_back(duc, dul, 1, zl * 8 + c)
        return carry

    lax.fori_loop(0, 8, send_grad_prod, 0)
    own_du = keep_back(duc, dul, 1)
    own_du.start()
    weight_term(3)
    def filter_sum(zz):
        wait_recv(frecv.at[0, pl.ds(0, 3 * ROWS), :], ss_f.at[0], rs_f.at[zz])
        total = fown[rows(zz, ROWS), :]
        for off in range(1, 4):
            total = total + frecv[lax.rem(x + off, 4), rows(zz, ROWS), :].astype(F32)
        return total

    for away in (2, 1, 3):
        zz = lax.rem(zh + away, 4)
        fsend2[zz] = filter_sum(zz).astype(BF16)
        remote(fsend2.at[zz], frecv2.at[zh], ss_f.at[1], rs_f.at[4], dp_dev(x, zz)).start()
    reduce_slab(3)
    grad = filter_sum(zh)

    own_qg.wait()
    own_du.wait()
    wait_recv(qgc.at[pl.ds(0, 15 * ROWS), :], ss_out.at[0], rs_out.at[0])
    wait_recv(qgc.at[pl.ds(0, 15 * ROWS), :], ss_out.at[1], rs_out.at[1])
    def branch_grads(i, carry):
        piece = cols(i)
        grad = dul[:, piece].astype(F32)
        value = (grad * kv[0, :, piece].astype(F32)).astype(BF16)
        kv[0, :, piece] = (grad * kv[1, :, piece].astype(F32)).astype(BF16)
        kv[1, :, piece] = value
        return carry

    lax.fori_loop(0, 16, branch_grads, 0)
    write_k = pltpu.make_async_copy(kv.at[0], kg_out, lsem.at[0])
    write_v = pltpu.make_async_copy(kv.at[1], vg_out, lsem.at[1])
    write_k.start()
    write_v.start()
    wait_recv(wrecv2.at[pl.ds(0, 3)], ss_w2.at[0], rs_w2.at[0])
    weight = wfin[...]
    for off in range(1, 4):
        weight = weight + wrecv2[lax.rem(zh + off, 4)].astype(F32)
    wg_out[...] = weight * (1.0 / 16.0)
    wait_recv(frecv2.at[pl.ds(0, 3)], ss_f.at[1], rs_f.at[4])
    for off in range(1, 4):
        grad = grad + frecv2[lax.rem(zh + off, 4)].astype(F32)
    fg_out[...] = grad * (1.0 / 16.0)

    write_k.wait()
    write_v.wait()
    for index in range(2):
        wait_send(uc.at[pl.ds(0, 15 * ROWS), :], ss_in.at[index], rs_in.at[index])
        wait_send(qgc.at[pl.ds(0, 15 * ROWS), :], ss_out.at[index], rs_out.at[index])
    wait_send(taps.at[pl.ds(0, 3 * ROWS), :], ss_par.at[0], rs_par.at[0])
    wait_send(wrows.at[0, pl.ds(0, 192), :], ss_par.at[1], rs_par.at[1])
    wait_send(taps.at[pl.ds(0, 3 * BLOCK), :], ss_par.at[2], rs_par.at[2])
    wait_send(wrows.at[pl.ds(0, 3)], ss_par.at[3], rs_par.at[3])

    def drain(part, carry):
        wait_send(cot.at[part, pl.ds(0, 15 * ROWS), :], ss_ag.at[part], rs_z.at[part])
        wait_send(wsend.at[part, pl.ds(0, 3)], ss_w.at[part], rs_w.at[part])
        return carry

    lax.fori_loop(0, PARTS, drain, 0)
    wait_send(wsend2.at[pl.ds(0, 3)], ss_w2.at[0], rs_w2.at[0])
    wait_send(fsend.at[pl.ds(0, 3)], ss_f.at[0], rs_f.at[0])
    wait_send(fsend2.at[pl.ds(0, 3)], ss_f.at[1], rs_f.at[4])


def hand_over(*refs):
    sources, targets, stage, (load_sem, store_sem) = refs[:5], refs[5:10], refs[10:15], refs[15:]
    loads, stores = [], []
    for i, source in enumerate(sources):
        parts = 2 if source.shape[1] == WIDTH else 1
        count = source.shape[0] // parts
        for part in range(parts):
            piece = pl.ds(part * count, count)
            n = len(loads)
            loads.append(pltpu.make_async_copy(source.at[piece], stage[i].at[piece], load_sem.at[n]))
            stores.append(pltpu.make_async_copy(stage[i].at[piece], targets[i].at[piece], store_sem.at[n]))
    for load in loads:
        load.start()
    for load, store in zip(loads, stores):
        load.wait()
        store.start()
    for store in stores:
        store.wait()


def shards(query_act, key_act, value_act, out_grad, out_weight, filter_taps):
    fwd, inv = transform_tables()
    anywhere = pl.BlockSpec(memory_space=pl.ANY)
    inside = pl.BlockSpec(memory_space=pltpu.VMEM)
    dma = pltpu.SemaphoreType.DMA

    def vmem(shape, dtype):
        return pltpu.VMEM(shape, dtype)

    outs = (
        jax.ShapeDtypeStruct((ROWS, WIDTH), BF16),
        jax.ShapeDtypeStruct((ROWS, WIDTH), BF16),
        jax.ShapeDtypeStruct((ROWS, WIDTH), BF16),
        jax.ShapeDtypeStruct((CHAN, PIECE), F32),
        jax.ShapeDtypeStruct((ROWS, CHAN), F32),
    )
    grads = pl.pallas_call(
        kernel,
        out_shape=outs,
        in_specs=[anywhere] * 8,
        out_specs=(anywhere, anywhere, anywhere, inside, inside),
        scratch_shapes=[
            vmem((2, ROWS, WIDTH), BF16),
            vmem((ROWS, WIDTH), BF16),
            vmem((2 * BLOCK, BLOCK), BF16),
            vmem((BLOCK, 2 * BLOCK), BF16),
            vmem((PARTS, SEQ, SLAB), BF16),
            vmem((PARTS, CHAN, SLAB), BF16),
            vmem((SEQ, CHAN), BF16),
            vmem((SEQ, CHAN), BF16),
            vmem((SEQ, CHAN), BF16),
            vmem((4, 2 * BLOCK, CHAN), F32),
            vmem((4, 2 * BLOCK, CHAN), F32),
            vmem((4, 2 * BLOCK, CHAN), F32),
            vmem((4, 2 * BLOCK, CHAN), BF16),
            vmem((SEQ, CHAN), F32),
            vmem((SEQ, CHAN), F32),
            vmem((CHAN, SEQ), BF16),
            vmem((SEQ, CHAN), BF16),
            vmem((SEQ, CHAN), BF16),
            vmem((ROWS, WIDTH), BF16),
            vmem((PARTS, 4, CHAN, PIECE), BF16),
            vmem((PARTS, 4, CHAN, PIECE), BF16),
            vmem((PARTS, CHAN, PIECE), F32),
            vmem((PARTS, CHAN, PIECE), BF16),
            vmem((4, CHAN, PIECE), BF16),
            vmem((CHAN, PIECE), F32),
            vmem((4, BLOCK, CHAN), BF16),
            vmem((4, BLOCK, CHAN), BF16),
            vmem((BLOCK, CHAN), F32),
            vmem((4, ROWS, CHAN), BF16),
            vmem((4, ROWS, CHAN), BF16),
            dma((11,)),
            dma((2,)), dma((2,)),
            dma((4,)), dma((8,)),
            dma((PARTS,)),
            *[dma((PARTS,)) for _ in range(9)],
            dma((PARTS,)), dma((PARTS,)),
            dma((1,)), dma((1,)),
            dma((2,)), dma((5,)),
            dma((2,)), dma((2,)),
        ],
        compiler_params=pltpu.CompilerParams(
            collective_id=0, has_side_effects=True, vmem_limit_bytes=60 * 1024 * 1024
        ),
        cost_estimate=pl.CostEstimate(flops=16_000_000_000, bytes_accessed=16_000_000, transcendentals=0),
        name="hyena_backward",
    )(query_act, key_act, value_act, out_grad, out_weight, filter_taps, fwd, inv)
    return pl.pallas_call(
        hand_over,
        out_shape=outs,
        in_specs=[anywhere] * 5,
        out_specs=(anywhere,) * 5,
        scratch_shapes=[vmem(out.shape, out.dtype) for out in outs] + [dma((8,)), dma((8,))],
        compiler_params=pltpu.CompilerParams(vmem_limit_bytes=60 * 1024 * 1024),
        cost_estimate=pl.CostEstimate(flops=0, bytes_accessed=7_000_000, transcendentals=0),
        name="hand_over",
    )(*grads)


def solution(mesh):
    return jax.shard_map(
        shards,
        mesh=mesh,
        in_specs=(
            P(("dp", "context"), None),
            P(("dp", "context"), None),
            P(("dp", "context"), None),
            P(("dp", "context"), None),
            P("context", "dp"),
            P("dp", "context"),
        ),
        out_specs=(
            P(("dp", "context"), None),
            P(("dp", "context"), None),
            P(("dp", "context"), None),
            P("context", "dp"),
            P("dp", "context"),
        ),
        check_vma=False,
    )
```

```python
import math

import jax
import jax.numpy as jnp
import numpy as np
from jax import lax
from jax.experimental import pallas as pl
from jax.experimental.pallas import tpu as pltpu
from jax.sharding import PartitionSpec as P

SEQ = 2048
CHAN = 256
ROWS = 128
WIDTH = 4096
BLOCK = 512
PARTS = 4
SLAB = 1024
PIECE = 256
HALF = 128
FAR_BY_PAIR = (0, 1, 2)
F32 = jnp.float32
BF16 = jnp.bfloat16
MESH = pl.DeviceIdType.MESH


def transform_tables():
    freq = np.concatenate([np.arange(0, BLOCK, 2), np.arange(1, BLOCK, 2)])
    time = np.arange(BLOCK)
    angle = ((2 * freq[:, None] + 1) * time[None, :] % (4 * BLOCK)) * (math.pi / (2 * BLOCK))
    table = np.concatenate([np.cos(angle), -np.sin(angle)], axis=0)
    return jnp.asarray(table, BF16), jnp.asarray(table.T / BLOCK, BF16)


def kernel(
    q_in, k_in, v_in, og_in, w_in, h_in, fwd_in, inv_in,
    qg_out, kg_out, vg_out, wg_out, fg_out,
    kv, ub, fwd, inv, cot, wrows, taps, qc, uc, spec_u, spec_g, spec_d, prod, zbuf, dgbuf, gtr, qgc, duc, dul,
    wsend, wrecv, wown, wsend2, wrecv2, wfin, fsend, frecv, fown, fsend2, frecv2,
    lsem, ss_in, rs_in, ss_par, rs_par, ss_ag, rs_z, rs_ym, rs_yp, rs_zym, rs_zyp, rs_far, rs_sib, rs_zfar, rs_zsib,
    ss_w, rs_w, ss_w2, rs_w2, ss_f, rs_f, ss_out, rs_out,
):
    dp = lax.axis_index("dp")
    ctx = lax.axis_index("context")
    x, zh = dp // 4, dp % 4
    zl, y, core = ctx // 8, (ctx // 2) % 4, ctx % 2

    def ctx_dev(c):
        return {"dp": dp, "context": c}

    def dp_dev(xx, zz):
        return {"dp": xx * 4 + zz, "context": ctx}

    def ctx_of(zz, yy, kk):
        return zz * 8 + lax.rem(yy + 4, 4) * 2 + kk

    def remote(src, dst, send, recv, dev):
        return pltpu.make_async_remote_copy(
            src_ref=src, dst_ref=dst, send_sem=send, recv_sem=recv, device_id=dev, device_id_type=MESH
        )

    me = ctx_dev(lax.rem(ctx + 1, 16))

    def wait_recv(ref, send, recv):
        remote(ref, ref, send, recv, me).wait_recv()

    def wait_send(ref, send, recv):
        remote(ref, ref, send, recv, me).wait_send()

    def cols(i):
        return pl.ds(pl.multiple_of(i * PIECE, PIECE), PIECE)

    def rows(i, n):
        return pl.ds(pl.multiple_of(i * n, n), n)

    local_k = pltpu.make_async_copy(k_in, kv.at[0], lsem.at[0])
    local_v = pltpu.make_async_copy(v_in, kv.at[1], lsem.at[1])
    local_k.start()
    local_v.start()
    def side_of(zz):
        return pl.ds(pl.multiple_of(x * PIECE + zz // 2 * HALF, HALF), HALF)

    local_w = [
        pltpu.make_async_copy(
            w_in.at[:, pl.ds(half * HALF, HALF)], wrows.at[lax.rem(zh, 2) * 2 + half, :, side_of(zh)], lsem.at[5]
        )
        for half in range(2)
    ]
    local_h = pltpu.make_async_copy(h_in, taps.at[rows(dp, ROWS), :], lsem.at[6])
    local_h.start()
    for copy in local_w:
        copy.start()
    local_q = pltpu.make_async_copy(q_in.at[:, cols(ctx)], qc.at[rows(ctx, ROWS), :], lsem.at[7])
    local_q.start()
    for part in range(PARTS):
        for xx in range(4):
            for side in range(2):
                pltpu.make_async_copy(
                    og_in.at[:, pl.ds((xx * 4 + part // 2 + 2 * side) * PIECE + part % 2 * HALF, HALF)],
                    cot.at[part, rows(ctx, ROWS), pl.ds(xx * PIECE + side * HALF, HALF)],
                    lsem.at[4],
                ).start()
    local_fwd = pltpu.make_async_copy(fwd_in, fwd, lsem.at[2])
    local_inv = pltpu.make_async_copy(inv_in, inv, lsem.at[3])
    local_fwd.start()
    local_inv.start()

    barrier = pltpu.get_barrier_semaphore()

    def greet(off, carry):
        pl.semaphore_signal(barrier, inc=1, device_id=ctx_dev(lax.rem(ctx + off, 16)), device_id_type=MESH)
        return carry

    lax.fori_loop(1, 16, greet, 0)
    for off in range(1, 4):
        pl.semaphore_signal(barrier, inc=1, device_id=dp_dev(lax.rem(x + off, 4), zh), device_id_type=MESH)
        pl.semaphore_signal(barrier, inc=1, device_id=dp_dev(x, lax.rem(zh + off, 4)), device_id_type=MESH)
    pl.semaphore_wait(barrier, 21)

    local_h.wait()
    z_up = dp_dev(x, lax.rem(zh + 1, 4))
    z_down = dp_dev(x, lax.rem(zh + 3, 4))

    def send_taps(zz, start, count, index, dev):
        piece = taps.at[pl.ds(pl.multiple_of((x * 4 + zz) * ROWS + start, 64), count), :]
        remote(piece, piece, ss_par.at[0], rs_par.at[index], dev).start()

    def send_rows(zz, start, count, index, dev):
        piece = wrows.at[pl.ds(lax.rem(zz, 2) * 2, 2), pl.ds(start, count), side_of(zz)]
        remote(piece, piece, ss_par.at[1], rs_par.at[index], dev).start()

    send_taps(zh, 0, ROWS, 0, z_up)
    send_taps(zh, 0, ROWS, 1, z_down)

    pltpu.make_async_copy(w_in, w_in, lsem.at[5]).wait()
    send_rows(zh, 0, CHAN, 3, z_up)
    send_rows(zh, 0, CHAN, 4, z_down)

    local_k.wait()
    local_v.wait()

    def product(i, carry):
        piece = cols(i)
        ub[:, piece] = (kv[0, :, piece].astype(F32) * kv[1, :, piece].astype(F32)).astype(BF16)
        return carry

    lax.fori_loop(0, 16, product, 0)
    local_u = pltpu.make_async_copy(ub.at[:, cols(ctx)], uc.at[rows(ctx, ROWS), :], lsem.at[8])
    local_u.start()

    dev_z = ctx_dev(ctx_of(1 - zl, y, core))
    dev_up = ctx_dev(ctx_of(zl, y + 1, core))
    dev_down = ctx_dev(ctx_of(zl, y - 1, core))
    dev_sib = ctx_dev(ctx_of(zl, y, 1 - core))

    def spread(part, c, start, count, recv, dev):
        piece = cot.at[part, pl.ds(pl.multiple_of(c * ROWS + start, 64), count), :]
        remote(piece, piece, ss_ag.at[part], recv.at[part], dev).start()

    def arrived(part, count, recv):
        wait_recv(cot.at[part, pl.ds(0, count), :], ss_ag.at[part], recv.at[part])

    def gather_own_z(part):
        spread(part, ctx, 0, ROWS, rs_z, dev_z)

    def gather_own_y(part):
        spread(part, ctx, 0, ROWS, rs_ym, dev_up)
        spread(part, ctx, 0, ROWS, rs_yp, dev_down)
        spread(part, ctx, 0, ROWS, rs_sib, dev_sib)

    def gather_pair(part):
        arrived(part, ROWS, rs_z)
        c = ctx_of(1 - zl, y, core)
        spread(part, c, 0, ROWS, rs_zym, dev_up)
        spread(part, c, 0, ROWS, rs_zyp, dev_down)
        spread(part, c, 0, ROWS, rs_zsib, dev_sib)

    def gather_near(part, own):
        zz = zl if own else 1 - zl
        from_down, from_up = (rs_ym, rs_yp) if own else (rs_zym, rs_zyp)
        far, sib = (rs_far, rs_sib) if own else (rs_zfar, rs_zsib)
        halves = own or part not in FAR_BY_PAIR
        arrived(part, ROWS, from_down)
        c = ctx_of(zz, y - 1, core)
        if halves:
            spread(part, c, 0, 64, far, dev_up)
        spread(part, c, 0, ROWS, sib, dev_sib)
        arrived(part, ROWS, from_up)
        c = ctx_of(zz, y + 1, core)
        if halves:
            spread(part, c, 64, 64, far, dev_down)
        spread(part, c, 0, ROWS, sib, dev_sib)

    def gather_far(part, own):
        zz = zl if own else 1 - zl
        far, sib = (rs_far, rs_sib) if own else (rs_zfar, rs_zsib)
        arrived(part, ROWS, far)
        c = ctx_of(zz, y + 2, core)
        if own and part in FAR_BY_PAIR:
            spread(part, c, 0, ROWS, rs_zfar, dev_z)
        spread(part, c, 0, ROWS, sib, dev_sib)

    def complete(part, own):
        arrived(part, 4 * ROWS, rs_sib if own else rs_zsib)

    pltpu.make_async_copy(cot.at[0, pl.ds(0, 512), :], cot.at[0, pl.ds(0, 512), :], lsem.at[4]).wait()
    gather_own_y(0)
    gather_own_y(1)
    gather_own_y(2)
    for start, recv, dev, away in ((0, 0, z_up, 3), (64, 1, z_down, 1)):
        wait_recv(taps.at[pl.ds(0, ROWS), :], ss_par.at[0], rs_par.at[recv])
        send_taps(lax.rem(zh + away, 4), start, 64, 2, dev)
    for start, recv, dev, away in ((0, 3, z_up, 3), (128, 4, z_down, 1)):
        wait_recv(wrows.at[0, pl.ds(0, 64), :], ss_par.at[1], rs_par.at[recv])
        send_rows(lax.rem(zh + away, 4), start, 128, 5, dev)

    def send_input(source, target, index):
        def step(off, carry):
            for zz in (1 - zl, zl):
                c = zz * 8 + lax.rem(ctx + off, 8)

                @pl.when(c != ctx)
                def _():
                    remote(
                        source.at[:, cols(c)], target.at[rows(ctx, ROWS), :], ss_in.at[index], rs_in.at[index], ctx_dev(c)
                    ).start()

            return carry

        lax.fori_loop(0, 8, step, 0)

    gather_own_z(0)
    send_input(ub, uc, 1)
    gather_own_z(1)
    gather_near(0, True)

    wait_recv(taps.at[pl.ds(0, ROWS), :], ss_par.at[0], rs_par.at[2])
    for off in range(1, 4):
        own = taps.at[rows(x, BLOCK), :]
        remote(own, own, ss_par.at[2], rs_par.at[6], dp_dev(lax.rem(x + off, 4), zh)).start()
    wait_recv(wrows.at[0, pl.ds(0, 64), :], ss_par.at[1], rs_par.at[5])
    for off in range(1, 4):
        own = wrows.at[:, :, cols(x)]
        remote(own, own, ss_par.at[3], rs_par.at[7], dp_dev(lax.rem(x + off, 4), zh)).start()
    gather_near(1, True)
    gather_pair(0)
    send_input(q_in, qc, 0)
    gather_near(2, True)

    def forward(source, spec, first, count):
        def step(j, carry):
            i = first + j
            spec[i] = jnp.dot(fwd[...], source[rows(i, BLOCK), :], preferred_element_type=F32)
            return carry

        lax.fori_loop(0, count, step, 0)

    def over_tiles(body):
        for half in range(2):
            sign = 1.0 - 2.0 * half

            def step(i, carry):
                base = pl.multiple_of(half * 256 + i * 16, 16)
                for lane in range(2):
                    body(pl.ds(base, 16), pl.ds(base + BLOCK, 16), pl.ds(lane * 128, 128), sign)
                return carry

            lax.fori_loop(0, 16, step, 0)

    local_fwd.wait()
    local_inv.wait()
    wait_recv(taps.at[pl.ds(0, 3 * BLOCK), :], ss_par.at[2], rs_par.at[6])
    forward(taps, spec_g, 0, 4)

    def window(re, im, lane, sign):
        for d in (3, 2, 1):
            real = spec_g[d, re, lane] - sign * spec_g[d - 1, im, lane]
            imag = spec_g[d, im, lane] + sign * spec_g[d - 1, re, lane]
            spec_g[d, re, lane] = real
            spec_g[d, im, lane] = imag

    over_tiles(window)

    local_u.wait()
    wait_recv(uc.at[pl.ds(0, 15 * ROWS), :], ss_in.at[1], rs_in.at[1])
    forward(uc, spec_u, 0, 4)

    def convolve(re, im, lane, sign):
        ure = [spec_u[a, re, lane] for a in range(4)]
        uim = [spec_u[a, im, lane] for a in range(4)]
        gre = [spec_g[a, re, lane] for a in range(4)]
        gim = [spec_g[a, im, lane] for a in range(4)]
        for i in range(4):
            prod[i, re, lane] = sum(ure[a] * gre[i - a] - uim[a] * gim[i - a] for a in range(i + 1)).astype(BF16)
            prod[i, im, lane] = sum(ure[a] * gim[i - a] + uim[a] * gre[i - a] for a in range(i + 1)).astype(BF16)

    over_tiles(convolve)
    def conv_out(i, carry):
        out = jnp.dot(inv[...], prod[i], preferred_element_type=F32)
        zbuf[rows(i, BLOCK), :] = out
        return carry

    gather_pair(1)
    gather_own_z(2)
    gather_own_z(3)
    lax.fori_loop(0, 4, conv_out, 0)
    local_q.wait()
    wait_recv(qc.at[pl.ds(0, 15 * ROWS), :], ss_in.at[0], rs_in.at[0])

    def gate(i, carry):
        block = rows(i, 256)
        gated = (qc[block, :].astype(F32) * zbuf[block, :]).astype(BF16).astype(F32)
        gtr[:, block] = gated.T.astype(BF16)
        dgbuf[block, :] = jnp.zeros((256, CHAN), F32)
        return carry

    lax.fori_loop(0, 8, gate, 0)

    def reduce_slab(part):
        wait_recv(wrecv.at[part, pl.ds(0, 3)], ss_w.at[part], rs_w.at[part])
        total = wown[part]
        for off in range(1, 4):
            total = total + wrecv[part, lax.rem(x + off, 4)].astype(F32)
        wsend2[part] = total.astype(BF16)
        target = pl.ds(part % 2 * HALF, HALF)
        for side in range(2):
            source = pl.ds(side * HALF, HALF)
            zz = part // 2 + 2 * side

            @pl.when(zh == zz)
            def _():
                wfin[:, target] = total[:, side * HALF : (side + 1) * HALF]

            @pl.when(zh != zz)
            def _():
                remote(
                    wsend2.at[part, :, source], wrecv2.at[zh, :, target], ss_w2.at[0], rs_w2.at[0], dp_dev(x, zz)
                ).start()

    def weight_term(part):
        def product_of(xx):
            return jnp.dot(gtr[...], cot[part, :, cols(xx)], preferred_element_type=F32)

        def step(off, carry):
            xx = lax.rem(x + off, 4)
            wsend[part, xx] = product_of(xx).astype(BF16)
            remote(wsend.at[part, xx], wrecv.at[part, x], ss_w.at[part], rs_w.at[part], dp_dev(xx, zh)).start()
            return carry

        lax.fori_loop(1, 4, step, 0)
        wown[part] = product_of(x)

    def grad_gated(part, own):
        zz = zl if own else 1 - zl

        def step(i, carry):
            block = rows(zz * 2 + i, BLOCK)
            dgbuf[block, :] += lax.dot_general(
                cot[part, block, :], wrows[part], (((1,), (1,)), ((), ())), preferred_element_type=F32
            )
            return carry

        lax.fori_loop(0, 2, step, 0)

    def send_back(source, target, index, c):
        @pl.when(c != ctx)
        def _():
            remote(
                source.at[rows(c, ROWS), :], target.at[:, cols(ctx)], ss_out.at[index], rs_out.at[index], ctx_dev(c)
            ).start()

    def keep_back(source, target, index):
        return pltpu.make_async_copy(source.at[rows(ctx, ROWS), :], target.at[:, cols(ctx)], lsem.at[9 + index])

    def finish_dg(own):
        zz = zl if own else 1 - zl

        def step(off, carry):
            c = zz * 8 + lax.rem(ctx + off, 8)
            block = rows(c, ROWS)
            grad = dgbuf[block, :]
            qgc[block, :] = (grad * zbuf[block, :]).astype(BF16)
            qc[block, :] = (grad * qc[block, :].astype(F32)).astype(BF16)
            send_back(qgc, qg_out, 0, c)
            return carry

        lax.fori_loop(0, 8, step, 0)
        forward(qc, spec_d, zz * 2, 2)

    gather_far(0, True)
    gather_far(1, True)
    gather_pair(2)
    gather_far(2, True)
    wait_recv(wrows.at[pl.ds(0, 3)], ss_par.at[3], rs_par.at[7])
    complete(0, True)
    grad_gated(0, True)
    gather_pair(3)
    complete(1, True)
    grad_gated(1, True)
    complete(2, True)
    grad_gated(2, True)
    gather_near(0, False)
    gather_far(0, False)
    gather_near(1, False)
    gather_near(2, False)
    complete(0, False)
    weight_term(0)
    grad_gated(0, False)
    gather_near(3, False)
    gather_own_y(3)
    gather_far(1, False)
    complete(1, False)
    weight_term(1)
    grad_gated(1, False)
    gather_far(2, False)
    gather_far(3, False)
    complete(2, False)
    grad_gated(2, False)
    complete(3, False)
    grad_gated(3, False)
    gather_near(3, True)
    finish_dg(False)
    reduce_slab(0)
    weight_term(2)
    gather_far(3, True)
    reduce_slab(1)
    complete(3, True)
    grad_gated(3, True)
    finish_dg(True)
    own_qg = keep_back(qgc, qg_out, 0)
    own_qg.start()
    reduce_slab(2)
    def filter_product(re, im, lane, sign):
        ure = [spec_u[a, re, lane] for a in range(4)]
        uim = [spec_u[a, im, lane] for a in range(4)]
        dre = [spec_d[a, re, lane] for a in range(4)]
        dim = [spec_d[a, im, lane] for a in range(4)]
        after = None
        for d in (3, 2, 1, 0):
            real = sum(ure[a] * dre[a + d] + uim[a] * dim[a + d] for a in range(4 - d))
            imag = sum(ure[a] * dim[a + d] - uim[a] * dre[a + d] for a in range(4 - d))
            if after is None:
                prod[d, re, lane] = real.astype(BF16)
                prod[d, im, lane] = imag.astype(BF16)
            else:
                prod[d, re, lane] = (real + sign * after[1]).astype(BF16)
                prod[d, im, lane] = (imag - sign * after[0]).astype(BF16)
            after = (real, imag)

    over_tiles(filter_product)

    def filter_of(xx):
        return jnp.dot(inv[...], prod[xx], preferred_element_type=F32)

    def filter_term(off, carry):
        xx = lax.rem(x + off, 4)
        fsend[xx] = filter_of(xx).astype(BF16)
        for away in (2, 1, 3, 0):
            zz = lax.rem(zh + away, 4)
            remote(
                fsend.at[xx, rows(zz, ROWS), :], frecv.at[x, rows(zz, ROWS), :], ss_f.at[0], rs_f.at[zz], dp_dev(xx, zh)
            ).start()
        return carry

    lax.fori_loop(1, 4, filter_term, 0)
    fown[...] = filter_of(x)

    def correlate(re, im, lane, sign):
        gre = [spec_g[a, re, lane] for a in range(4)]
        gim = [spec_g[a, im, lane] for a in range(4)]
        dre = [spec_d[a, re, lane] for a in range(4)]
        dim = [spec_d[a, im, lane] for a in range(4)]
        for a in range(4):
            prod[a, re, lane] = sum(gre[i - a] * dre[i] + gim[i - a] * dim[i] for i in range(a, 4)).astype(BF16)
            prod[a, im, lane] = sum(gre[i - a] * dim[i] - gim[i - a] * dre[i] for i in range(a, 4)).astype(BF16)

    over_tiles(correlate)

    def grad_prod(i, carry):
        duc[rows(i, BLOCK), :] = jnp.dot(inv[...], prod[i], preferred_element_type=F32).astype(BF16)
        return carry

    lax.fori_loop(0, 4, grad_prod, 0)

    def send_grad_prod(off, carry):
        c = lax.rem(ctx + off, 8)
        send_back(duc, dul, 1, (1 - zl) * 8 + c)
        send_back(duc, dul, 1, zl * 8 + c)
        return carry

    lax.fori_loop(0, 8, send_grad_prod, 0)
    own_du = keep_back(duc, dul, 1)
    own_du.start()
    weight_term(3)
    def filter_sum(zz):
        wait_recv(frecv.at[0, pl.ds(0, 3 * ROWS), :], ss_f.at[0], rs_f.at[zz])
        total = fown[rows(zz, ROWS), :]
        for off in range(1, 4):
            total = total + frecv[lax.rem(x + off, 4), rows(zz, ROWS), :].astype(F32)
        return total

    for away in (2, 1, 3):
        zz = lax.rem(zh + away, 4)
        fsend2[zz] = filter_sum(zz).astype(BF16)
        remote(fsend2.at[zz], frecv2.at[zh], ss_f.at[1], rs_f.at[4], dp_dev(x, zz)).start()
    reduce_slab(3)
    grad = filter_sum(zh)

    own_qg.wait()
    own_du.wait()
    wait_recv(qgc.at[pl.ds(0, 15 * ROWS), :], ss_out.at[0], rs_out.at[0])
    wait_recv(qgc.at[pl.ds(0, 15 * ROWS), :], ss_out.at[1], rs_out.at[1])
    def branch_grads(i, carry):
        piece = cols(i)
        grad = dul[:, piece].astype(F32)
        value = (grad * kv[0, :, piece].astype(F32)).astype(BF16)
        kv[0, :, piece] = (grad * kv[1, :, piece].astype(F32)).astype(BF16)
        kv[1, :, piece] = value
        return carry

    lax.fori_loop(0, 16, branch_grads, 0)
    write_k = pltpu.make_async_copy(kv.at[0], kg_out, lsem.at[0])
    write_v = pltpu.make_async_copy(kv.at[1], vg_out, lsem.at[1])
    write_k.start()
    write_v.start()
    wait_recv(wrecv2.at[pl.ds(0, 3)], ss_w2.at[0], rs_w2.at[0])
    weight = wfin[...]
    for off in range(1, 4):
        weight = weight + wrecv2[lax.rem(zh + off, 4)].astype(F32)
    wg_out[...] = weight * (1.0 / 16.0)
    wait_recv(frecv2.at[pl.ds(0, 3)], ss_f.at[1], rs_f.at[4])
    for off in range(1, 4):
        grad = grad + frecv2[lax.rem(zh + off, 4)].astype(F32)
    fg_out[...] = grad * (1.0 / 16.0)

    write_k.wait()
    write_v.wait()
    for index in range(2):
        wait_send(uc.at[pl.ds(0, 15 * ROWS), :], ss_in.at[index], rs_in.at[index])
        wait_send(qgc.at[pl.ds(0, 15 * ROWS), :], ss_out.at[index], rs_out.at[index])
    wait_send(taps.at[pl.ds(0, 3 * ROWS), :], ss_par.at[0], rs_par.at[0])
    wait_send(wrows.at[0, pl.ds(0, 192), :], ss_par.at[1], rs_par.at[1])
    wait_send(taps.at[pl.ds(0, 3 * BLOCK), :], ss_par.at[2], rs_par.at[2])
    wait_send(wrows.at[pl.ds(0, 3)], ss_par.at[3], rs_par.at[3])

    def drain(part, carry):
        wait_send(cot.at[part, pl.ds(0, 15 * ROWS), :], ss_ag.at[part], rs_z.at[part])
        wait_send(wsend.at[part, pl.ds(0, 3)], ss_w.at[part], rs_w.at[part])
        return carry

    lax.fori_loop(0, PARTS, drain, 0)
    wait_send(wsend2.at[pl.ds(0, 3)], ss_w2.at[0], rs_w2.at[0])
    wait_send(fsend.at[pl.ds(0, 3)], ss_f.at[0], rs_f.at[0])
    wait_send(fsend2.at[pl.ds(0, 3)], ss_f.at[1], rs_f.at[4])


def hand_over(*refs):
    sources, targets, stage, (load_sem, store_sem) = refs[:5], refs[5:10], refs[10:15], refs[15:]
    loads, stores = [], []
    for i, source in enumerate(sources):
        parts = 4 if source.shape[1] == WIDTH else 1
        count = source.shape[0] // parts
        for part in range(parts):
            piece = pl.ds(part * count, count)
            n = len(loads)
            loads.append(pltpu.make_async_copy(source.at[piece], stage[i].at[piece], load_sem.at[n]))
            stores.append(pltpu.make_async_copy(stage[i].at[piece], targets[i].at[piece], store_sem.at[n]))
    for load in loads:
        load.start()
    for load, store in zip(loads, stores):
        load.wait()
        store.start()
    for store in stores:
        store.wait()


def shards(query_act, key_act, value_act, out_grad, out_weight, filter_taps):
    fwd, inv = transform_tables()
    anywhere = pl.BlockSpec(memory_space=pl.ANY)
    inside = pl.BlockSpec(memory_space=pltpu.VMEM)
    dma = pltpu.SemaphoreType.DMA

    def vmem(shape, dtype):
        return pltpu.VMEM(shape, dtype)

    outs = (
        jax.ShapeDtypeStruct((ROWS, WIDTH), BF16),
        jax.ShapeDtypeStruct((ROWS, WIDTH), BF16),
        jax.ShapeDtypeStruct((ROWS, WIDTH), BF16),
        jax.ShapeDtypeStruct((CHAN, PIECE), F32),
        jax.ShapeDtypeStruct((ROWS, CHAN), F32),
    )
    grads = pl.pallas_call(
        kernel,
        out_shape=outs,
        in_specs=[anywhere] * 8,
        out_specs=(anywhere, anywhere, anywhere, inside, inside),
        scratch_shapes=[
            vmem((2, ROWS, WIDTH), BF16),
            vmem((ROWS, WIDTH), BF16),
            vmem((2 * BLOCK, BLOCK), BF16),
            vmem((BLOCK, 2 * BLOCK), BF16),
            vmem((PARTS, SEQ, SLAB), BF16),
            vmem((PARTS, CHAN, SLAB), BF16),
            vmem((SEQ, CHAN), BF16),
            vmem((SEQ, CHAN), BF16),
            vmem((SEQ, CHAN), BF16),
            vmem((4, 2 * BLOCK, CHAN), F32),
            vmem((4, 2 * BLOCK, CHAN), F32),
            vmem((4, 2 * BLOCK, CHAN), F32),
            vmem((4, 2 * BLOCK, CHAN), BF16),
            vmem((SEQ, CHAN), F32),
            vmem((SEQ, CHAN), F32),
            vmem((CHAN, SEQ), BF16),
            vmem((SEQ, CHAN), BF16),
            vmem((SEQ, CHAN), BF16),
            vmem((ROWS, WIDTH), BF16),
            vmem((PARTS, 4, CHAN, PIECE), BF16),
            vmem((PARTS, 4, CHAN, PIECE), BF16),
            vmem((PARTS, CHAN, PIECE), F32),
            vmem((PARTS, CHAN, PIECE), BF16),
            vmem((4, CHAN, PIECE), BF16),
            vmem((CHAN, PIECE), F32),
            vmem((4, BLOCK, CHAN), BF16),
            vmem((4, BLOCK, CHAN), BF16),
            vmem((BLOCK, CHAN), F32),
            vmem((4, ROWS, CHAN), BF16),
            vmem((4, ROWS, CHAN), BF16),
            dma((11,)),
            dma((2,)), dma((2,)),
            dma((4,)), dma((8,)),
            dma((PARTS,)),
            *[dma((PARTS,)) for _ in range(9)],
            dma((PARTS,)), dma((PARTS,)),
            dma((1,)), dma((1,)),
            dma((2,)), dma((5,)),
            dma((2,)), dma((2,)),
        ],
        compiler_params=pltpu.CompilerParams(
            collective_id=0, has_side_effects=True, vmem_limit_bytes=60 * 1024 * 1024
        ),
        cost_estimate=pl.CostEstimate(flops=16_000_000_000, bytes_accessed=16_000_000, transcendentals=0),
        name="hyena_backward",
    )(query_act, key_act, value_act, out_grad, out_weight, filter_taps, fwd, inv)
    return pl.pallas_call(
        hand_over,
        out_shape=outs,
        in_specs=[anywhere] * 5,
        out_specs=(anywhere,) * 5,
        scratch_shapes=[vmem(out.shape, out.dtype) for out in outs] + [dma((14,)), dma((14,))],
        compiler_params=pltpu.CompilerParams(vmem_limit_bytes=60 * 1024 * 1024),
        cost_estimate=pl.CostEstimate(flops=0, bytes_accessed=7_000_000, transcendentals=0),
        name="hand_over",
    )(*grads)


def solution(mesh):
    return jax.shard_map(
        shards,
        mesh=mesh,
        in_specs=(
            P(("dp", "context"), None),
            P(("dp", "context"), None),
            P(("dp", "context"), None),
            P(("dp", "context"), None),
            P("context", "dp"),
            P("dp", "context"),
        ),
        out_specs=(
            P(("dp", "context"), None),
            P(("dp", "context"), None),
            P(("dp", "context"), None),
            P("context", "dp"),
            P("dp", "context"),
        ),
        check_vma=False,
    )
```
